256 devices in a mesh: row: 16 (over z, core), col: 16 (over y, x).
Axes of the slice: x: 4, y: 4, z: 8, core: 2. Of those that a mesh axis runs over, the one named last changes fastest.
Arguments:
- feats: bfloat16 [32768, 256], P(('row', 'col')), may hold values from -6 to 6
- tiles: bfloat16 [256, 192, 128, 128], P(('row', 'col')), may hold values from 0.099609375 to 1
- tile_row: int32 [256, 192], P(('row', 'col')), may hold values from 0 to 15
- tile_col: int32 [256, 192], P(('row', 'col')), may hold values from 0 to 15
- counts: int32 [256], P(('row', 'col')), may hold values from 48 to 192, as said below
- w_self: bfloat16 [256, 256], replicated, may hold values from -0.375 to 0.375
- w_neigh: bfloat16 [256, 256], replicated, may hold values from -0.375 to 0.375
- bias: float32 [256], replicated, may hold values from -4 to 4
- grad_out: bfloat16 [32768, 256], P(('row', 'col')), may hold values from -6 to 6
Outputs:
- output: bfloat16 [32768, 256], P(('row', 'col'))
- d_feats: bfloat16 [32768, 256], P(('row', 'col'))
- d_wself: float32 [256, 256], replicated
- d_wneigh: float32 [256, 256], replicated
- d_bias: float32 [256], replicated
The draws below stay inside these ranges and needn't reach their ends.
Inputs may be any that keep to these rules, and one draw needn't show every extreme that they name: `counts`: each device uses between a quarter of its 192 slots and all of them; some device uses all.
All inputs are finite; a program needn't handle non-finite values.
Results may differ from the reference program's by a relative error of at most 0.019.
Values may be sent and summed in bfloat16 or wider, within the bound.
A program may use at most 128 MiB of HBM per device.

```python
import math
import jax
import jax.numpy as jnp
from jax import lax

F = 256
TILE = 128
NODE_DEV = 128
NODES = 32768
MAXT = 192
N_ROW = 16
N_COL = 16


def draw_counts(key, part):
    key = jax.random.fold_in(key, 7)
    used = jax.random.randint(key, (N_ROW * N_COL,), MAXT // 4, MAXT + 1).astype(jnp.int32)
    chosen = jax.random.randint(jax.random.fold_in(key, 11), (), 0, N_ROW * N_COL)
    return used.at[chosen].set(MAXT).astype(jnp.int32)


def touch_ends(array, rng, smallest, top_value):
    place = [jax.random.randint(jax.random.fold_in(rng, axis), (), 0, length) for axis, length in enumerate(array.shape)]
    main_axis = array.shape.index(max(array.shape))
    neighbour = place[:main_axis] + [(place[main_axis] + 1) % array.shape[main_axis]] + place[main_axis + 1:]
    return array.at[tuple(place)].set(smallest).at[tuple(neighbour)].set(top_value)


def level_of(rng, shape, shards, low, largest):
    def one(position, parts):
        heights = jax.random.uniform(jax.random.fold_in(jax.random.fold_in(rng, 6), position), (parts,), jnp.float32, low / len(shards), largest / len(shards))
        return jnp.repeat(jnp.exp(heights), shape[position] // parts).reshape((-1,) + (1,) * (len(shape) - position - 1))

    level = one(*shards[0])
    for cut in shards[1:]:
        level = level * one(*cut)
    return level


def gaussian(key, dims, width, most, shards=(), kind=jnp.bfloat16):
    entries = jax.random.normal(key, dims, jnp.float32) * width
    if len(shards) > 0:
        entries = level_of(key, dims, shards, -0.22, 0.18) * entries
    return jnp.clip(entries, min=-most, max=most).astype(kind)


def setup_inputs(seed: int = 0) -> dict:
    splits = jax.random.split(jax.random.key(seed), 10)
    return {
        "feats": gaussian(splits[0], (NODES, F), 1.0, 6.0, ((0, 256),)),
        "tiles": jnp.clip(jnp.exp(math.log(1.0) - 2.306499 * jax.random.uniform(splits[1], (N_ROW * N_COL, MAXT, TILE, TILE), jnp.float32) ** level_of(splits[1], (N_ROW * N_COL, MAXT, TILE, TILE), ((0, 256),), -0.2, 0.2)), 0.099609375, 1.0).astype(jnp.bfloat16),
        "tile_row": touch_ends(jax.random.randint(splits[2], (N_ROW * N_COL, MAXT), 0, NODE_DEV * N_COL // TILE), jax.random.fold_in(splits[2], 1), 0, (NODE_DEV * N_COL // TILE) - 1).astype(jnp.int32),
        "tile_col": touch_ends(jax.random.randint(splits[3], (N_ROW * N_COL, MAXT), 0, NODE_DEV * N_ROW // TILE), jax.random.fold_in(splits[3], 1), 0, (NODE_DEV * N_ROW // TILE) - 1).astype(jnp.int32),
        "counts": draw_counts(jax.random.fold_in(splits[9], 71), 0),
        "w_self": gaussian(splits[5], (F, F), F ** -0.5, 0.375),
        "w_neigh": gaussian(splits[6], (F, F), F ** -0.5, 0.375),
        "bias": gaussian(splits[7], (F,), 1.0, 4.0, (), jnp.float32),
        "grad_out": gaussian(splits[8], (NODES, F), 1.0, 6.0, ((0, 256),)),
    }


def reference(feats, tiles, tile_row, tile_col, counts, w_self, w_neigh, bias, grad_out):
    row_tiles = NODE_DEV * N_COL // TILE
    col_tiles = NODE_DEV * N_ROW // TILE
    grid_feats = feats.reshape(N_ROW, N_COL, NODE_DEV, F)
    col_blocks = jnp.transpose(grid_feats, (1, 0, 2, 3)).reshape(N_COL, col_tiles, TILE, F)
    slot_ids = jnp.arange(MAXT, dtype=jnp.int32)
    device_ids = jnp.arange(N_ROW * N_COL, dtype=jnp.int32)

    def masked_tiles(device):
        usable = slot_ids < counts[device]
        return jnp.where(usable[:, None, None], tiles[device], jnp.zeros((), tiles.dtype)).astype(jnp.float32)

    def forward_step(state_pair, device):
        sums_all, degree_all = state_pair
        block_row = device // N_COL
        block_col = device % N_COL
        masked = masked_tiles(device)
        operand = col_blocks[block_col][tile_col[device]].astype(jnp.float32)
        product = jnp.einsum('tij,tjf->tif', masked, operand, precision=lax.Precision.HIGHEST)
        term_rows = jax.ops.segment_sum(product, tile_row[device], num_segments=row_tiles)
        term_degree = jax.ops.segment_sum(lax.optimization_barrier(jnp.sum(masked, axis=2)), tile_row[device], num_segments=row_tiles)
        sums_all = sums_all.at[block_row].add(term_rows)
        degree_all = degree_all.at[block_row].add(term_degree)
        return ((sums_all, degree_all), None)
    start_sums = jnp.zeros((N_ROW, row_tiles, TILE, F), jnp.float32)
    start_degree = jnp.zeros((N_ROW, row_tiles, TILE), jnp.float32)
    (summed, degree), _ = lax.scan(forward_step, (start_sums, start_degree), device_ids)
    summed = summed.reshape(NODES, F)
    degree = degree.reshape(NODES)
    scaling = lax.rsqrt(1.0 + degree)[:, None]
    mixed = (summed * scaling).astype(jnp.bfloat16)
    pre = jnp.dot(feats, w_self, preferred_element_type=jnp.float32) + jnp.dot(mixed, w_neigh, preferred_element_type=jnp.float32) + bias
    sigmoid_val = jax.nn.sigmoid(pre)
    output = (pre * sigmoid_val).astype(jnp.bfloat16)
    slope = sigmoid_val * (1.0 + pre * (1.0 - sigmoid_val))
    grad_pre = (grad_out.astype(jnp.float32) * slope).astype(jnp.bfloat16)
    d_wself = jnp.dot(feats.T, grad_pre, preferred_element_type=jnp.float32)
    d_wneigh = jnp.dot(mixed.T, grad_pre, preferred_element_type=jnp.float32)
    d_bias = lax.optimization_barrier(jnp.sum(grad_pre.astype(jnp.float32), axis=0))
    back_rows = (jnp.dot(grad_pre, w_neigh.T, preferred_element_type=jnp.float32) * scaling).astype(jnp.bfloat16)
    self_grad = jnp.dot(grad_pre, w_self.T, preferred_element_type=jnp.float32)
    row_blocks = back_rows.reshape(N_ROW, row_tiles, TILE, F)

    def backward_step(back_all, device):
        block_row = device // N_COL
        block_col = device % N_COL
        masked = masked_tiles(device)
        operand = row_blocks[block_row][tile_row[device]].astype(jnp.float32)
        product = jnp.einsum('tij,tif->tjf', masked, operand, precision=lax.Precision.HIGHEST)
        term_cols = jax.ops.segment_sum(product, tile_col[device], num_segments=col_tiles)
        return (back_all.at[block_col].add(term_cols), None)
    start_back = jnp.zeros((N_COL, col_tiles, TILE, F), jnp.float32)
    back_all, _ = lax.scan(backward_step, start_back, device_ids)
    back_all = jnp.transpose(back_all.reshape(N_COL, N_ROW, NODE_DEV, F), (1, 0, 2, 3)).reshape(NODES, F)
    d_feats = (self_grad + back_all).astype(jnp.bfloat16)
    return (output, d_feats, d_wself, d_wneigh, d_bias)
```

```python
import jax
import jax.numpy as jnp
from jax import lax
from jax.experimental import pallas as pl
from jax.experimental.pallas import tpu as pltpu
from jax.sharding import PartitionSpec as P

MESH = pl.DeviceIdType.MESH
F32 = jnp.float32
BF16 = jnp.bfloat16
NZ, NY, NX = 8, 4, 4
NC = NY * NX
NR = 2 * NZ
T = 128
F = 256
SLOTS = 192
TILE_CUTS = 6
CUT = SLOTS // TILE_CUTS
PART = F // NZ
WPART = PART + 16
NT = (((1,), (1,)), ((), ()))
TN = (((0,), (0,)), ((), ()))


def layer_kernel(
    feats, tiles, tile_row, tile_col, counts, w_self, w_neigh, bias, grad_out,
    out, d_feats, d_wself, d_wneigh, d_bias,
    tiles_v, run, tab_v, tab, a_ref, at_ref, acc, x_all, part, part_in, degs, deg_in, pre_self, own_sum,
    back_all, sib_out, sib_in, comb, comb_in, grads, grads_in, w1_out, w1_in, w2_in, w3, w3_in, self_grad,
    tile_sem, tab_sem, agz_s, agz_r, sib_s, sib_r, deg_s, deg_r, rs_s, rs_r, ag_s, ag_r, bs_s, bs_r, rz_s, rz_r,
    w0_s, w0_r, w1_s, w1_r, w2_s, w2_r, w3_s, w3_r, w4_s, w4_r,
):
    row = lax.axis_index("row")
    col = lax.axis_index("col")
    z, k = row // 2, row % 2
    y, x = col // NX, col % NX
    sibling = (z * 2 + (1 - k), col)

    def z_to(d):
        return (((z + d) % NZ) * 2 + k, col)

    def xy_index(p):
        return ((y + p // NX) % NY) * NX + (x + p % NX) % NX

    def xy_from(p):
        return ((y + NY - p // NX) % NY) * NX + (x + NX - p % NX) % NX

    def loop(lower, upper, body):
        def step(i, carry):
            body(i)
            return carry

        lax.fori_loop(lower, upper, step, 0)

    def remote(src, dst, send, recv, where):
        return pltpu.make_async_remote_copy(
            src_ref=src, dst_ref=dst, send_sem=send, recv_sem=recv, device_id=where, device_id_type=MESH
        )

    def tile_copy(i):
        cut = pl.ds(i * CUT, CUT)
        return pltpu.make_async_copy(tiles.at[cut], tiles_v.at[cut], tile_sem.at[i])

    for i in range(TILE_CUTS):
        tile_copy(i).start()

    barrier = pltpu.get_barrier_semaphore()
    pl.semaphore_signal(barrier, inc=1, device_id=sibling, device_id_type=MESH)
    loop(1, NZ, lambda d: pl.semaphore_signal(barrier, inc=1, device_id=z_to(d), device_id_type=MESH))
    loop(1, NC, lambda p: pl.semaphore_signal(barrier, inc=1, device_id=(row, xy_index(p)), device_id_type=MESH))

    key_row = tile_row[...] * NR + tile_col[...]
    lane = lax.broadcasted_iota(jnp.int32, (1, SLOTS), 1)
    key_row = jnp.where(lane < counts[0], key_row, 4096)
    first = lax.broadcasted_iota(jnp.int32, (SLOTS, SLOTS), 0)
    second = lax.broadcasted_iota(jnp.int32, (SLOTS, SLOTS), 1)
    keys = jnp.broadcast_to(key_row, (SLOTS, SLOTS))
    key_col = jnp.sum(jnp.where(first == second, keys, 0), axis=1, keepdims=True)
    before = jnp.max(jnp.where((key_col == keys) & (first < second), first, -1), axis=0, keepdims=True)
    place = lax.broadcasted_iota(jnp.int32, (SLOTS, F), 1)
    slot = lax.broadcasted_iota(jnp.int32, (SLOTS, F), 0)
    last = jnp.max(jnp.where(key_col == place, slot, -1), axis=0, keepdims=True)
    tab_v[0:1, 0:SLOTS] = jnp.where(before < 0, SLOTS, before)
    tab_v[1:2, :] = jnp.where(last < 0, SLOTS, last)
    tab_copy = pltpu.make_async_copy(tab_v, tab, tab_sem)
    tab_copy.start()
    x_all[row] = feats[...]
    run[SLOTS] = jnp.zeros((T, T), F32)
    pl.semaphore_wait(barrier, 1 + (NZ - 1) + (NC - 1))

    def agz(d):
        return remote(feats, x_all.at[row], agz_s.at[d], agz_r.at[d], z_to(d))

    def near_first(i):
        return jnp.where(i % 2 == 1, (i + 1) // 2, NZ - i // 2)

    loop(1, NZ, lambda i: agz(NZ - near_first(i)).start())

    def to_sibling(zp):
        return remote(x_all.at[zp * 2 + k], x_all.at[zp * 2 + k], sib_s.at[zp], sib_r.at[zp], sibling)

    to_sibling(z).start()

    tab_copy.wait()
    for i in range(TILE_CUTS):
        tile_copy(i).wait()

        def add_up(s):
            run[s] = run[tab[0, s]] + tiles_v[s].astype(F32)

        loop(i * CUT, (i + 1) * CUT, add_up)

    def assemble(c):
        rows = pl.ds(pl.multiple_of(c * T, T), T)
        total = jnp.zeros((T, T), F32)
        for r in range(NR):
            block = run[tab[1, c * NR + r]]
            total = total + block
            a_ref[r // 2, rows, (r % 2) * T : (r % 2 + 1) * T] = block.astype(BF16)
        degs[c] = lax.dot_general(
            jnp.ones((8, T), F32), total, NT, preferred_element_type=F32, precision=lax.Precision.HIGHEST
        )

    loop(0, NC, assemble)

    def send_degree(p):
        return remote(degs.at[xy_index(p)], deg_in.at[p], deg_s.at[p], deg_r.at[p], (row, xy_index(p)))

    loop(1, NC, lambda p: send_degree(p).start())

    def multiply(matrix, index, right, add):
        def chunk(m):
            rows = pl.ds(pl.multiple_of(m * 512, 512), 512)
            term = jnp.dot(matrix[index, rows, :], right, preferred_element_type=F32)
            acc[rows, :] = acc[rows, :] + term if add else term

        loop(0, 4, chunk)

    def pair_of(ref, i):
        return jnp.concatenate([ref[2 * i], ref[2 * i + 1]], axis=0)

    to_sibling(z).wait_recv()
    multiply(a_ref, z, pair_of(x_all, z), False)

    def arrive(i):
        d = near_first(i)
        agz(d).wait_recv()
        to_sibling((z + NZ - d) % NZ).start()

    arrive(1)

    def forward(i):
        arrive(i + 1)
        zp = (z + NZ - near_first(i)) % NZ
        to_sibling(zp).wait_recv()
        multiply(a_ref, zp, pair_of(x_all, zp), True)

    loop(1, NZ - 1, forward)
    z_last = (z + NZ - NZ // 2) % NZ
    to_sibling(z_last).wait_recv()

    def send_part(p):
        return remote(part.at[xy_index(p)], part_in.at[p], rs_s.at[p], rs_r.at[p], (row, xy_index(p)))

    x_last = pair_of(x_all, z_last)

    def finish(p):
        c = xy_index(p)
        rows = pl.ds(pl.multiple_of(c * T, T), T)
        return acc[rows, :] + jnp.dot(a_ref[z_last, rows, :], x_last, preferred_element_type=F32)

    def finish_send(i):
        p = (i + 9) % (NC - 1) + 1
        part[xy_index(p)] = finish(p).astype(BF16)
        send_part(p).start()

    loop(0, NC - 1, finish_send)
    own_sum[...] = finish(0)

    def turn(q):
        for e in range(2):
            rows = pl.ds(pl.multiple_of((2 * q + e) * T, T), T)
            for r in range(NR):
                at_ref[q, r * T : (r + 1) * T, e * T : (e + 1) * T] = a_ref[
                    r // 2, rows, (r % 2) * T : (r % 2 + 1) * T
                ].T

    loop(0, NC // 2, turn)
    pre_self[...] = jnp.dot(feats[...], w_self[...], preferred_element_type=F32) + bias[...]

    own_degree = degs[col]
    for p in range(1, NC):
        send_degree(p).wait_recv()
        own_degree = own_degree + deg_in[p]
    scale_row = lax.rsqrt(1.0 + own_degree[0:1, :])
    scale = jnp.broadcast_to(scale_row, (T, T)).T
    scale = jnp.concatenate([scale, scale], axis=1)

    def take_part(i):
        p = (i + 9) % (NC - 1) + 1
        send_part(p).wait_recv()
        own_sum[...] = own_sum[...] + part_in[p].astype(F32)

    loop(0, NC - 1, take_part)

    mixed = (own_sum[...] * scale).astype(BF16)
    pre = pre_self[...] + jnp.dot(mixed, w_neigh[...], preferred_element_type=F32)
    sig = 1.0 / (1.0 + jnp.exp(-pre))
    slope = sig * (1.0 + pre * (1.0 - sig))
    grad_pre = (grad_out[...].astype(F32) * slope).astype(BF16)
    back = lax.dot_general(grad_pre, w_neigh[...], NT, preferred_element_type=F32) * scale
    back_all[col] = back.astype(BF16)

    def send_back(p):
        return remote(back_all.at[col], back_all.at[col], ag_s.at[p], ag_r.at[p], (row, xy_index(p)))

    loop(0, NC - 1, lambda i: send_back((i + 9) % (NC - 1) + 1).start())
    out[...] = (pre * sig).astype(BF16)

    bias_sum = jnp.sum(grad_pre.astype(F32), axis=0, keepdims=True)
    grads[0, 0:F, :] = lax.dot_general(feats[...], grad_pre, TN, preferred_element_type=F32)
    grads[1, 0:F, :] = lax.dot_general(mixed, grad_pre, TN, preferred_element_type=F32)
    grads[0, F : F + 8, :] = jnp.broadcast_to(bias_sum, (8, F))
    grads[1, F : F + 8, :] = jnp.broadcast_to(bias_sum, (8, F))
    w0 = remote(grads.at[1 - k], grads_in, w0_s, w0_r, sibling)
    w0.start()
    self_grad[...] = lax.dot_general(grad_pre, w_self[...], NT, preferred_element_type=F32)
    w0.wait_recv()
    bias_two = (grads[k, F : F + 8, :] + grads_in[F : F + 8, :])[0:1, :]

    def send_w1(d):
        zp = (z + d) % NZ
        return remote(w1_out.at[zp], w1_in.at[z], w1_s.at[d], w1_r.at[d], z_to(d))

    for zp in range(NZ):
        rows = slice(zp * PART, (zp + 1) * PART)
        w1_out[zp, 0:PART, :] = (grads[k, rows, :] + grads_in[rows, :]).astype(BF16)
        w1_out[zp, PART:WPART, :] = jnp.broadcast_to(bias_two, (16, F)).astype(BF16)
    loop(1, NZ, lambda d: send_w1(d).start())
    w1_in[z] = w1_out[z]

    def await_pair(q):
        yp = (y + q // 2) % NY
        for e in range(2):
            xp = ((x // 2 + q % 2) % 2) * 2 + e
            send_back(((y + NY - yp) % NY) * NX + (x + NX - xp) % NX).wait_recv()
        return yp * 2 + (x // 2 + q % 2) % 2

    send_back((NX + x - (x + 1 - 2 * (x % 2))) % NX).wait_recv()
    multiply(at_ref, col // 2, pair_of(back_all, col // 2), False)

    def backward(q):
        index = await_pair(q)
        multiply(at_ref, index, pair_of(back_all, index), True)

    loop(1, 6, backward)

    def send_w2(p):
        return remote(w2_in.at[col], w2_in.at[col], w2_s.at[p], w2_r.at[p], (row, xy_index(p)))

    loop(1, NZ, lambda d: send_w1(d).wait_recv())
    w1_sum = w1_in[0].astype(F32)
    for zp in range(1, NZ):
        w1_sum = w1_sum + w1_in[zp].astype(F32)
    w2_in[col] = w1_sum.astype(BF16)
    loop(1, NC, lambda p: send_w2(p).start())

    backward(6)
    b_index = await_pair(7)
    b_last = pair_of(back_all, b_index)

    def finish_back(r):
        rows = pl.ds(pl.multiple_of(r * T, T), T)
        return acc[rows, :] + jnp.dot(at_ref[b_index, rows, :], b_last, preferred_element_type=F32)

    def far_first(i):
        return near_first(NZ - 1 - i)

    def to_sibling_back(zp):
        return remote(sib_out.at[zp], sib_in.at[zp], bs_s.at[zp], bs_r.at[zp], sibling)

    def give_sibling(i):
        zp = (z + far_first(i)) % NZ
        sib_out[zp] = finish_back(zp * 2 + 1 - k).astype(BF16)
        to_sibling_back(zp).start()

    loop(0, NZ, give_sibling)

    def send_comb(d):
        zp = (z + d) % NZ
        return remote(comb.at[zp], comb_in.at[d], rz_s.at[d], rz_r.at[d], z_to(d))

    def combine(zp):
        to_sibling_back(zp).wait_recv()
        return finish_back(zp * 2 + k) + sib_in[zp].astype(F32)

    def combine_send(i):
        d = far_first(i)
        zp = (z + d) % NZ
        comb[zp] = combine(zp).astype(BF16)
        send_comb(d).start()

    loop(0, NZ - 1, combine_send)
    own_sum[...] = combine(z) + self_grad[...]

    loop(1, NC, lambda p: send_w2(p).wait_recv())
    w2_sum = w2_in[0].astype(F32)
    for c in range(1, NC):
        w2_sum = w2_sum + w2_in[c].astype(F32)
    d_bias[...] = w2_sum[PART : PART + 1, :]
    w3[z] = w2_sum[0:PART, :].astype(BF16)

    def send_w3(d):
        return remote(w3.at[z], w3.at[z], w3_s.at[d], w3_r.at[d], z_to(d))

    loop(1, NZ, lambda d: send_w3(d).start())

    def take_comb(i):
        d = far_first(i)
        send_comb(d).wait_recv()
        own_sum[...] = own_sum[...] + comb_in[d].astype(F32)

    loop(0, NZ - 1, take_comb)
    d_feats[...] = own_sum[...].astype(BF16)

    loop(1, NZ, lambda d: send_w3(d).wait_recv())
    w4 = remote(w3, w3_in, w4_s, w4_r, sibling)
    w4.start()
    w4.wait_recv()
    core = jnp.full((F, F), k, jnp.int32)
    mine = w3[...].reshape(F, F).astype(F32)
    other = w3_in[...].reshape(F, F).astype(F32)
    d_wself[...] = jnp.where(core == 0, mine, other)
    d_wneigh[...] = jnp.where(core == 0, other, mine)

    def sent_z(d):
        agz(d).wait_send()
        send_w1(d).wait_send()
        send_comb(d).wait_send()
        send_w3(d).wait_send()

    loop(1, NZ, sent_z)

    def sent_xy(p):
        send_degree(p).wait_send()
        send_part(p).wait_send()
        send_back(p).wait_send()
        send_w2(p).wait_send()

    loop(1, NC, sent_xy)

    def sent_sibling(zp):
        to_sibling(zp).wait_send()
        to_sibling_back(zp).wait_send()

    loop(0, NZ, sent_sibling)
    w0.wait_send()
    w4.wait_send()


def per_device(feats, tiles, tile_row, tile_col, counts, w_self, w_neigh, bias, grad_out):
    vmem = pl.BlockSpec(memory_space=pltpu.VMEM)
    dma = pltpu.SemaphoreType.DMA
    outs = pl.pallas_call(
        layer_kernel,
        out_shape=(
            jax.ShapeDtypeStruct((T, F), BF16),
            jax.ShapeDtypeStruct((T, F), BF16),
            jax.ShapeDtypeStruct((F, F), F32),
            jax.ShapeDtypeStruct((F, F), F32),
            jax.ShapeDtypeStruct((1, F), F32),
        ),
        in_specs=[
            vmem,
            pl.BlockSpec(memory_space=pl.ANY),
            vmem,
            vmem,
            pl.BlockSpec(memory_space=pltpu.SMEM),
            vmem,
            vmem,
            vmem,
            vmem,
        ],
        out_specs=(vmem,) * 5,
        scratch_shapes=[
            pltpu.VMEM((SLOTS, T, T), BF16),
            pltpu.VMEM((SLOTS + 1, T, T), F32),
            pltpu.VMEM((8, F), jnp.int32),
            pltpu.SMEM((8, F), jnp.int32),
            pltpu.VMEM((NZ, NC * T, 2 * T), BF16),
            pltpu.VMEM((NC // 2, NR * T, 2 * T), BF16),
            pltpu.VMEM((NC * T, F), F32),
            pltpu.VMEM((NR, T, F), BF16),
            pltpu.VMEM((NC, T, F), BF16),
            pltpu.VMEM((NC, T, F), BF16),
            pltpu.VMEM((NC, 8, T), F32),
            pltpu.VMEM((NC, 8, T), F32),
            pltpu.VMEM((T, F), F32),
            pltpu.VMEM((T, F), F32),
            pltpu.VMEM((NC, T, F), BF16),
            pltpu.VMEM((NZ, T, F), BF16),
            pltpu.VMEM((NZ, T, F), BF16),
            pltpu.VMEM((NZ, T, F), BF16),
            pltpu.VMEM((NZ, T, F), BF16),
            pltpu.VMEM((2, F + 8, F), F32),
            pltpu.VMEM((F + 8, F), F32),
            pltpu.VMEM((NZ, WPART, F), BF16),
            pltpu.VMEM((NZ, WPART, F), BF16),
            pltpu.VMEM((NC, WPART, F), BF16),
            pltpu.VMEM((NZ, PART, F), BF16),
            pltpu.VMEM((NZ, PART, F), BF16),
            pltpu.VMEM((T, F), F32),
            dma((TILE_CUTS,)),
            dma,
        ]
        + [dma((NZ,))] * 4
        + [dma((NC,))] * 6
        + [dma((NZ,))] * 4
        + [dma, dma]
        + [dma((NZ,))] * 2
        + [dma((NC,))] * 2
        + [dma((NZ,))] * 2
        + [dma, dma],
        compiler_params=pltpu.CompilerParams(
            collective_id=0, has_side_effects=True, vmem_limit_bytes=56 * 2**20
        ),
        name="sage_layer",
    )(
        feats,
        tiles.reshape(SLOTS, T, T),
        tile_row,
        tile_col,
        counts,
        w_self,
        w_neigh,
        bias.reshape(1, F),
        grad_out,
    )
    return (outs[0], outs[1], outs[2], outs[3], outs[4].reshape(F))


def solution(mesh):
    placed = (
        P(("row", "col"), None),
        P(("row", "col"), None, None, None),
        P(("row", "col"), None),
        P(("row", "col"), None),
        P(("row", "col")),
        P(),
        P(),
        P(),
        P(("row", "col"), None),
    )
    return jax.shard_map(
        per_device,
        mesh=mesh,
        in_specs=placed,
        out_specs=(P(("row", "col"), None), P(("row", "col"), None), P(), P(), P()),
        check_vma=False,
    )
```

```python
import jax
import jax.numpy as jnp
from jax import lax
from jax.experimental import pallas as pl
from jax.experimental.pallas import tpu as pltpu
from jax.sharding import PartitionSpec as P

MESH = pl.DeviceIdType.MESH
F32 = jnp.float32
BF16 = jnp.bfloat16
NZ, NY, NX = 8, 4, 4
NC = NY * NX
NR = 2 * NZ
T = 128
F = 256
SLOTS = 192
TILE_CUTS = 6
CUT = SLOTS // TILE_CUTS
PART = F // NZ
HALF = T // 2
WPART = PART + 16
NT = (((1,), (1,)), ((), ()))
TN = (((0,), (0,)), ((), ()))


def first_legs():
    legs = []
    for du, dv in ((2, 2), (1, 1), (3, 3), (2, 1), (1, 2), (3, 1), (1, 3), (2, 3), (3, 2), (0, 2), (1, 0), (3, 0)):
        if (du + dv) % 2 == 0:
            relay, along, across = (0, dv), dv, du
        else:
            relay, along, across = (du, 0), du, dv
        line = across // 2 if across % 2 == 0 else 2 + across // 2
        legs.append((du, dv, *relay, line * 4 + (4 - along) % 4))
    return tuple(legs)


FIRST_LEG = first_legs()
LINES = ((2, 0), (0, 1), (0, 3))
OWN_WAYS = ((1, 0), (2, 0), (3, 0), (0, 1), (0, 2), (0, 3))
PAIRS = (
    ((0, 0), (2, 0)),
    ((0, 1), (0, 3)),
    ((1, 0), (3, 0)),
    ((0, 2), (2, 2)),
    ((1, 1), (3, 1)),
    ((1, 3), (3, 3)),
    ((2, 1), (2, 3)),
    ((1, 2), (3, 2)),
)
Z_ORDER = (4, 3, 5, 1, 7, 2, 6, 0)


def pick(i, values):
    chosen = values[0]
    for n, value in enumerate(values[1:], 1):
        chosen = jnp.where(i == n, value, chosen)
    return chosen


def layer_kernel(
    feats, tiles, tile_row, tile_col, counts, w_self, w_neigh, bias, grad_out,
    out, d_feats, d_wself, d_wneigh, d_bias,
    tiles_v, run, tab_v, tab, a_ref, at_ref, acc, x_all, part, part_in, line_sum, line_in, degs, deg_in, pre_self, own_sum,
    back_all, sib_out, sib_in, comb, far_in, half_in, comb_in, grads, grads_in, w1_out, w1_in, w2_in, w3, w3_in, self_grad,
    tile_sem, tab_sem, agz_s, agz_r, sib_s, sib_r, deg_s, deg_r, rs_s, rs_r, rl_s, rl_r, ag_s, ag_r, bs_s, bs_r, rz_s, rz_r,
    w0_s, w0_r, w1_s, w1_r, w2_s, w2_r, w3_s, w3_r, w4_s, w4_r,
):
    row = lax.axis_index("row")
    col = lax.axis_index("col")
    z, k = row // 2, row % 2
    y, x = col // NX, col % NX
    sibling = (z * 2 + (1 - k), col)

    def z_to(d):
        return (((z + d) % NZ) * 2 + k, col)

    def xy_index(p):
        return ((y + p // NX) % NY) * NX + (x + p % NX) % NX

    odd = (x + y) % 2

    def at(du, dv):
        yp = (y + (1 - odd) * du + odd * dv) % NY
        return yp * NX + (x + odd * du + (1 - odd) * dv) % NX

    def loop(lower, upper, body):
        def step(i, carry):
            body(i)
            return carry

        lax.fori_loop(lower, upper, step, 0)

    def remote(src, dst, send, recv, where):
        return pltpu.make_async_remote_copy(
            src_ref=src, dst_ref=dst, send_sem=send, recv_sem=recv, device_id=where, device_id_type=MESH
        )

    def tile_copy(i):
        cut = pl.ds(i * CUT, CUT)
        return pltpu.make_async_copy(tiles.at[cut], tiles_v.at[cut], tile_sem.at[i])

    for i in range(TILE_CUTS):
        tile_copy(i).start()

    barrier = pltpu.get_barrier_semaphore()
    pl.semaphore_signal(barrier, inc=1, device_id=sibling, device_id_type=MESH)
    loop(1, NZ, lambda d: pl.semaphore_signal(barrier, inc=1, device_id=z_to(d), device_id_type=MESH))
    loop(1, NC, lambda p: pl.semaphore_signal(barrier, inc=1, device_id=(row, xy_index(p)), device_id_type=MESH))

    key_row = tile_row[...] * NR + tile_col[...]
    lane = lax.broadcasted_iota(jnp.int32, (1, SLOTS), 1)
    key_row = jnp.where(lane < counts[0], key_row, 4096)
    first = lax.broadcasted_iota(jnp.int32, (SLOTS, SLOTS), 0)
    second = lax.broadcasted_iota(jnp.int32, (SLOTS, SLOTS), 1)
    keys = jnp.broadcast_to(key_row, (SLOTS, SLOTS))
    key_col = jnp.sum(jnp.where(first == second, keys, 0), axis=1, keepdims=True)
    before = jnp.max(jnp.where((key_col == keys) & (first < second), first, -1), axis=0, keepdims=True)
    place = lax.broadcasted_iota(jnp.int32, (SLOTS, F), 1)
    slot = lax.broadcasted_iota(jnp.int32, (SLOTS, F), 0)
    last = jnp.max(jnp.where(key_col == place, slot, -1), axis=0, keepdims=True)
    tab_v[0:1, 0:SLOTS] = jnp.where(before < 0, SLOTS, before)
    tab_v[1:2, :] = jnp.where(last < 0, SLOTS, last)
    tab_copy = pltpu.make_async_copy(tab_v, tab, tab_sem)
    tab_copy.start()
    x_all[row] = feats[...]
    run[SLOTS] = jnp.zeros((T, T), F32)
    pl.semaphore_wait(barrier, 1 + (NZ - 1) + (NC - 1))

    def near(side, hops):
        sign = 1 - 2 * side
        return remote(
            feats, x_all.at[row], agz_s.at[2 * hops + side - 2], agz_r.at[2 * hops + side - 2], z_to(NZ + sign * hops)
        )

    def passed(side):
        sign = 1 - 2 * side
        block = x_all.at[((z + NZ - 2 * sign) % NZ) * 2 + k]
        return remote(block, block, agz_s.at[4 + side], agz_r.at[4 + side], z_to(NZ + sign))

    def passed_half(side):
        sign = 1 - 2 * side
        block = x_all.at[((z + NZ - 2 * sign) % NZ) * 2 + k, pl.ds(side * HALF, HALF)]
        return remote(block, block, agz_s.at[6 + side], agz_r.at[6 + side], z_to(NZ + 2 * sign))

    for hops in (2, 1):
        for side in range(2):
            near(side, hops).start()

    def to_sibling(zp):
        return remote(x_all.at[zp * 2 + k], x_all.at[zp * 2 + k], sib_s.at[zp], sib_r.at[zp], sibling)

    to_sibling(z).start()

    tab_copy.wait()
    for i in range(TILE_CUTS):
        tile_copy(i).wait()

        def add_up(s):
            run[s] = run[tab[0, s]] + tiles_v[s].astype(F32)

        loop(i * CUT, (i + 1) * CUT, add_up)

    def assemble(c):
        rows = pl.ds(pl.multiple_of(c * T, T), T)
        total = jnp.zeros((T, T), F32)
        for r in range(NR):
            block = run[tab[1, c * NR + r]]
            total = total + block
            a_ref[r // 2, rows, (r % 2) * T : (r % 2 + 1) * T] = block.astype(BF16)
        degs[c] = lax.dot_general(
            jnp.ones((8, T), F32), total, NT, preferred_element_type=F32, precision=lax.Precision.HIGHEST
        )

    loop(0, NC // 2, assemble)
    for side in range(2):
        sign = 1 - 2 * side
        near(side, 2).wait_recv()
        passed_half(side).start()
        passed(side).start()
        to_sibling((z + NZ - 2 * sign) % NZ).start()
    loop(NC // 2, NC, assemble)

    def send_degree(p):
        return remote(degs.at[xy_index(p)], deg_in.at[p], deg_s.at[p], deg_r.at[p], (row, xy_index(p)))

    loop(1, NC, lambda p: send_degree(p).start())

    def multiply(left, right, add):
        term = jnp.dot(left, right, preferred_element_type=F32)
        acc[...] = acc[...] + term if add else term

    def pair_of(ref, i):
        return jnp.concatenate([ref[2 * i], ref[2 * i + 1]], axis=0)

    for side in range(2):
        near(side, 1).wait_recv()
        to_sibling((z + NZ - (1 - 2 * side)) % NZ).start()
    to_sibling(z).wait_recv()
    multiply(a_ref[z], pair_of(x_all, z), False)

    def forward(i):
        zp = (z + pick(i, (6, 2, 7, 1, 5, 3))) % NZ
        to_sibling(zp).wait_recv()
        multiply(a_ref[zp], pair_of(x_all, zp), True)

    loop(0, 4, forward)
    for side in range(2):
        passed(side).wait_recv()
        to_sibling((z + NZ - 3 * (1 - 2 * side)) % NZ).start()
    z_last = (z + NZ // 2) % NZ
    for side in range(2):
        block = x_all.at[z_last * 2 + k, pl.ds(side * HALF, HALF)]
        remote(block, block, agz_s.at[6 + side], agz_r.at[6 + side], sibling).wait_recv()
    to_sibling(z_last).start()
    loop(4, 6, forward)
    to_sibling(z_last).wait_recv()

    def send_part(du, dv, relay, slot, sem):
        return remote(part.at[at(du, dv)], part_in.at[slot], rs_s.at[sem], rs_r.at[slot], (row, at(*relay)))

    def took_part(slot):
        return remote(part_in.at[slot], part_in.at[slot], rs_s.at[0], rs_r.at[slot], sibling).wait_recv()

    x_last = pair_of(x_all, z_last)

    def finish(c):
        rows = pl.ds(pl.multiple_of(c * T, T), T)
        return acc[rows, :] + jnp.dot(a_ref[z_last, rows, :], x_last, preferred_element_type=F32)

    def part_copy(i):
        du, dv, ru, rv, slot = (pick(i, values) for values in zip(*FIRST_LEG))
        return du, dv, send_part(du, dv, (ru, rv), slot, i)

    def finish_send(i):
        du, dv, copy = part_copy(i)
        part[at(du, dv)] = finish(at(du, dv)).astype(BF16)
        copy.start()

    loop(0, len(FIRST_LEG), finish_send)

    def finish_line(j):
        du, dv = (pick(j - 1, values) for values in zip(*LINES))
        own_rows = pl.ds(pl.multiple_of(at(du, dv) * T, T), T)
        acc[own_rows, :] = finish(at(du, dv))

    loop(1, 4, finish_line)
    own_sum[...] = finish(col)

    def turn(c):
        rows = pl.ds(pl.multiple_of(c * T, T), T)
        for r in range(NR):
            at_ref[c, r * T : (r + 1) * T, :] = a_ref[r // 2, rows, (r % 2) * T : (r % 2 + 1) * T].T

    loop(0, NC // 2, turn)

    def send_line(j):
        du, dv = (pick(j - 1, values) for values in zip(*LINES))
        slot = pick(j - 1, (2, 3, 1))
        return remote(line_sum.at[j], line_in.at[slot], rl_s.at[j], rl_r.at[slot], (row, at(du, dv)))

    def add_line(j):
        du, dv = (pick(j - 1, values) for values in zip(*LINES))
        rows = pl.ds(pl.multiple_of(at(du, dv) * T, T), T)
        total = acc[rows, :]
        for e in range(1, 4):
            took_part(4 * j + e)
            total = total + part_in[4 * j + e].astype(F32)
        line_sum[j] = total.astype(BF16)
        send_line(j).start()

    loop(1, 4, add_line)
    loop(NC // 2, NC, turn)
    pre_self[...] = jnp.dot(feats[...], w_self[...], preferred_element_type=F32) + bias[...]

    own_degree = degs[col]
    for p in range(1, NC):
        send_degree(p).wait_recv()
        own_degree = own_degree + deg_in[p]
    scale_row = lax.rsqrt(1.0 + own_degree[0:1, :])
    scale = jnp.broadcast_to(scale_row, (T, T)).T
    scale = jnp.concatenate([scale, scale], axis=1)

    for e in range(1, 4):
        took_part(e)
        own_sum[...] = own_sum[...] + part_in[e].astype(F32)
    for e in range(1, 4):
        remote(line_in.at[e], line_in.at[e], rl_s.at[0], rl_r.at[e], sibling).wait_recv()
        own_sum[...] = own_sum[...] + line_in[e].astype(F32)

    mixed = (own_sum[...] * scale).astype(BF16)
    pre = pre_self[...] + jnp.dot(mixed, w_neigh[...], preferred_element_type=F32)
    sig = 1.0 / (1.0 + jnp.exp(-pre))
    slope = sig * (1.0 + pre * (1.0 - sig))
    grad_pre = (grad_out[...].astype(F32) * slope).astype(BF16)
    back = lax.dot_general(grad_pre, w_neigh[...], NT, preferred_element_type=F32) * scale
    back_all[col] = back.astype(BF16)

    def send_back(source, du, dv, sem):
        return remote(back_all.at[source], back_all.at[source], ag_s.at[sem], ag_r.at[source], (row, at(du, dv)))

    def own_back(i):
        du, dv = (pick(i, values) for values in zip(*OWN_WAYS))
        return send_back(col, du, dv, i)

    def took_back(source):
        remote(back_all.at[source], back_all.at[source], ag_s.at[0], ag_r.at[source], sibling).wait_recv()

    def pass_back(f, e):
        du, dv = LINES[f]
        source = at(du, dv)
        return send_back(source, *((0, e) if f == 0 else (e, 0)), 3 + 3 * f + 2 + e)

    loop(0, len(OWN_WAYS), lambda i: own_back(i).start())
    out[...] = (pre * sig).astype(BF16)

    bias_sum = jnp.sum(grad_pre.astype(F32), axis=0, keepdims=True)
    grads[0, 0:F, :] = lax.dot_general(feats[...], grad_pre, TN, preferred_element_type=F32)
    grads[1, 0:F, :] = lax.dot_general(mixed, grad_pre, TN, preferred_element_type=F32)
    grads[0, F : F + 8, :] = jnp.broadcast_to(bias_sum, (8, F))
    grads[1, F : F + 8, :] = jnp.broadcast_to(bias_sum, (8, F))
    w0 = remote(grads.at[1 - k], grads_in, w0_s, w0_r, sibling)
    w0.start()
    self_grad[...] = lax.dot_general(grad_pre, w_self[...], NT, preferred_element_type=F32)
    w0.wait_recv()
    bias_two = (grads[k, F : F + 8, :] + grads_in[F : F + 8, :])[0:1, :]

    def send_w1(d):
        zp = (z + d) % NZ
        return remote(w1_out.at[zp], w1_in.at[z], w1_s.at[d], w1_r.at[d], z_to(d))

    for zp in range(NZ):
        rows = slice(zp * PART, (zp + 1) * PART)
        w1_out[zp, 0:PART, :] = (grads[k, rows, :] + grads_in[rows, :]).astype(BF16)
        w1_out[zp, PART:WPART, :] = jnp.broadcast_to(bias_two, (16, F)).astype(BF16)
    loop(1, NZ, lambda d: send_w1(d).start())
    w1_in[z] = w1_out[z]

    for f in range(3):
        took_back(at(*LINES[f]))
        loop(1, 4, lambda e: pass_back(f, e).start())

    def pair_at(i):
        return tuple(at(*(pick(i, values) for values in zip(*(pair[n] for pair in PAIRS)))) for n in range(2))

    def two_of(ref, a, b, axis):
        return jnp.concatenate([ref[a], ref[b]], axis=axis)

    a, b = pair_at(0)
    multiply(two_of(at_ref, a, b, 1), two_of(back_all, a, b, 0), False)

    def backward(i):
        a, b = pair_at(i)
        pl.when(i > 1)(lambda: took_back(a))
        pl.when((i > 1))(lambda: took_back(b))
        multiply(two_of(at_ref, a, b, 1), two_of(back_all, a, b, 0), True)

    loop(1, 5, backward)

    def send_w2(p):
        return remote(w2_in.at[col], w2_in.at[col], w2_s.at[p], w2_r.at[p], (row, xy_index(p)))

    loop(1, NZ, lambda d: send_w1(d).wait_recv())
    w1_sum = w1_in[0].astype(F32)
    for zp in range(1, NZ):
        w1_sum = w1_sum + w1_in[zp].astype(F32)
    w2_in[col] = w1_sum.astype(BF16)
    loop(1, NC, lambda p: send_w2(p).start())

    loop(5, 7, backward)
    b_first, b_second = pair_at(7)
    took_back(b_first)
    took_back(b_second)
    b_last = two_of(back_all, b_first, b_second, 0)

    def finish_back(r):
        rows = pl.ds(pl.multiple_of(r * T, T), T)
        left = jnp.concatenate([at_ref[b_first, rows, :], at_ref[b_second, rows, :]], axis=1)
        return acc[rows, :] + jnp.dot(left, b_last, preferred_element_type=F32)

    def to_sibling_back(zp):
        return remote(sib_out.at[zp], sib_in.at[zp], bs_s.at[zp], bs_r.at[zp], sibling)

    def give_sibling(i):
        zp = (z + pick(i, Z_ORDER)) % NZ
        sib_out[zp] = finish_back(zp * 2 + 1 - k).astype(BF16)
        to_sibling_back(zp).start()

    loop(0, NZ, give_sibling)

    def combine(zp):
        to_sibling_back(zp).wait_recv()
        return finish_back(zp * 2 + k) + sib_in[zp].astype(F32)

    def send_half(side):
        sign = 1 - 2 * side
        half = comb.at[(z + NZ // 2) % NZ, pl.ds(side * HALF, HALF)]
        return remote(half, half_in.at[side], rz_s.at[side], rz_r.at[side], z_to(NZ - 2 * sign))

    def send_far(side):
        sign = 1 - 2 * side
        block = comb.at[(z + NZ - 3 * sign) % NZ]
        return remote(block, far_in.at[side], rz_s.at[2 + side], rz_r.at[2 + side], z_to(NZ - sign))

    def send_comb(side, hops):
        sign = 1 - 2 * side
        slot = 2 * (hops - 1) + side
        block = comb.at[(z + NZ - hops * sign) % NZ]
        return remote(block, comb_in.at[slot], rz_s.at[4 + slot], rz_r.at[4 + slot], z_to(NZ - hops * sign))

    z_four = (z + NZ // 2) % NZ
    comb[z_four] = combine(z_four).astype(BF16)
    for side in range(2):
        send_half(side).start()
    for side in range(2):
        zp = (z + NZ - 3 * (1 - 2 * side)) % NZ
        comb[zp] = combine(zp).astype(BF16)
        send_far(side).start()
    for side in range(2):
        zp = (z + NZ - (1 - 2 * side)) % NZ
        comb[zp] = combine(zp).astype(BF16)
        send_comb(side, 1).start()
    own_sum[...] = combine(z) + self_grad[...]
    for side in range(2):
        zp = (z + NZ - 2 * (1 - 2 * side)) % NZ
        total = combine(zp)
        send_far(side).wait_recv()
        total = total + far_in[side].astype(F32)
        send_half(side).wait_recv()
        added = half_in[side].astype(F32)
        zeros = jnp.zeros((HALF, F), F32)
        total = total + jnp.concatenate([zeros, added] if side else [added, zeros], axis=0)
        comb[zp] = total.astype(BF16)
        send_comb(side, 2).start()

    loop(1, NC, lambda p: send_w2(p).wait_recv())
    w2_sum = w2_in[0].astype(F32)
    for c in range(1, NC):
        w2_sum = w2_sum + w2_in[c].astype(F32)
    d_bias[...] = w2_sum[PART : PART + 1, :]
    w3[z] = w2_sum[0:PART, :].astype(BF16)

    def send_w3(d):
        return remote(w3.at[z], w3.at[z], w3_s.at[d], w3_r.at[d], z_to(d))

    loop(1, NZ, lambda d: send_w3(d).start())

    for hops in (1, 2):
        for side in range(2):
            send_comb(side, hops).wait_recv()
            own_sum[...] = own_sum[...] + comb_in[2 * (hops - 1) + side].astype(F32)
    d_feats[...] = own_sum[...].astype(BF16)

    loop(1, NZ, lambda d: send_w3(d).wait_recv())
    w4 = remote(w3, w3_in, w4_s, w4_r, sibling)
    w4.start()
    w4.wait_recv()
    core = jnp.full((F, F), k, jnp.int32)
    mine = w3[...].reshape(F, F)
    other = w3_in[...].reshape(F, F)
    d_wself[...] = jnp.where(core == 0, mine, other)
    d_wneigh[...] = jnp.where(core == 0, other, mine)

    for side in range(2):
        near(side, 1).wait_send()
        near(side, 2).wait_send()
        passed(side).wait_send()
        passed_half(side).wait_send()
        send_half(side).wait_send()
        send_far(side).wait_send()
        send_comb(side, 1).wait_send()
        send_comb(side, 2).wait_send()

    def sent_z(d):
        send_w1(d).wait_send()
        send_w3(d).wait_send()

    loop(1, NZ, sent_z)

    def sent_xy(p):
        send_degree(p).wait_send()
        send_w2(p).wait_send()

    loop(1, NC, sent_xy)
    loop(0, len(FIRST_LEG), lambda i: part_copy(i)[2].wait_send())
    loop(1, 4, lambda j: send_line(j).wait_send())
    loop(0, len(OWN_WAYS), lambda i: own_back(i).wait_send())
    for f in range(3):
        loop(1, 4, lambda e: pass_back(f, e).wait_send())

    def sent_sibling(zp):
        to_sibling(zp).wait_send()
        to_sibling_back(zp).wait_send()

    loop(0, NZ, sent_sibling)
    w0.wait_send()
    w4.wait_send()


def hand_over(*refs):
    for source, target in zip(refs[:5], refs[5:]):
        target[...] = source[...].astype(target.dtype)


def per_device(feats, tiles, tile_row, tile_col, counts, w_self, w_neigh, bias, grad_out):
    vmem = pl.BlockSpec(memory_space=pltpu.VMEM)
    dma = pltpu.SemaphoreType.DMA
    outs = pl.pallas_call(
        layer_kernel,
        out_shape=(
            jax.ShapeDtypeStruct((T, F), BF16),
            jax.ShapeDtypeStruct((T, F), BF16),
            jax.ShapeDtypeStruct((F, F), BF16),
            jax.ShapeDtypeStruct((F, F), BF16),
            jax.ShapeDtypeStruct((1, F), F32),
        ),
        in_specs=[
            vmem,
            pl.BlockSpec(memory_space=pl.ANY),
            vmem,
            vmem,
            pl.BlockSpec(memory_space=pltpu.SMEM),
            vmem,
            vmem,
            vmem,
            vmem,
        ],
        out_specs=(vmem,) * 5,
        scratch_shapes=[
            pltpu.VMEM((SLOTS, T, T), BF16),
            pltpu.VMEM((SLOTS + 1, T, T), F32),
            pltpu.VMEM((8, F), jnp.int32),
            pltpu.SMEM((8, F), jnp.int32),
            pltpu.VMEM((NZ, NC * T, 2 * T), BF16),
            pltpu.VMEM((NC, NR * T, T), BF16),
            pltpu.VMEM((NC * T, F), F32),
            pltpu.VMEM((NR, T, F), BF16),
            pltpu.VMEM((NC, T, F), BF16),
            pltpu.VMEM((NC, T, F), BF16),
            pltpu.VMEM((4, T, F), BF16),
            pltpu.VMEM((4, T, F), BF16),
            pltpu.VMEM((NC, 8, T), F32),
            pltpu.VMEM((NC, 8, T), F32),
            pltpu.VMEM((T, F), F32),
            pltpu.VMEM((T, F), F32),
            pltpu.VMEM((NC, T, F), BF16),
            pltpu.VMEM((NZ, T, F), BF16),
            pltpu.VMEM((NZ, T, F), BF16),
            pltpu.VMEM((NZ, T, F), BF16),
            pltpu.VMEM((2, T, F), BF16),
            pltpu.VMEM((2, HALF, F), BF16),
            pltpu.VMEM((4, T, F), BF16),
            pltpu.VMEM((2, F + 8, F), F32),
            pltpu.VMEM((F + 8, F), F32),
            pltpu.VMEM((NZ, WPART, F), BF16),
            pltpu.VMEM((NZ, WPART, F), BF16),
            pltpu.VMEM((NC, WPART, F), BF16),
            pltpu.VMEM((NZ, PART, F), BF16),
            pltpu.VMEM((NZ, PART, F), BF16),
            pltpu.VMEM((T, F), F32),
            dma((TILE_CUTS,)),
            dma,
        ]
        + [dma((NZ,))] * 4
        + [dma((NC,))] * 4
        + [dma((4,))] * 2
        + [dma((NC,))] * 2
        + [dma((NZ,))] * 4
        + [dma, dma]
        + [dma((NZ,))] * 2
        + [dma((NC,))] * 2
        + [dma((NZ,))] * 2
        + [dma, dma],
        compiler_params=pltpu.CompilerParams(
            collective_id=0, has_side_effects=True, vmem_limit_bytes=56 * 2**20
        ),
        name="sage_layer",
    )(
        feats,
        tiles.reshape(SLOTS, T, T),
        tile_row,
        tile_col,
        counts,
        w_self,
        w_neigh,
        bias.reshape(1, F),
        grad_out,
    )
    outs = pl.pallas_call(
        hand_over,
        out_shape=[jax.ShapeDtypeStruct(o.shape, t) for o, t in zip(outs, (BF16, BF16, F32, F32, F32))],
        in_specs=[vmem] * 5,
        out_specs=[vmem] * 5,
        name="hand_over",
    )(*outs)
    return (outs[0], outs[1], outs[2], outs[3], outs[4].reshape(F))


def solution(mesh):
    placed = (
        P(("row", "col"), None),
        P(("row", "col"), None, None, None),
        P(("row", "col"), None),
        P(("row", "col"), None),
        P(("row", "col")),
        P(),
        P(),
        P(),
        P(("row", "col"), None),
    )
    return jax.shard_map(
        per_device,
        mesh=mesh,
        in_specs=placed,
        out_specs=(P(("row", "col"), None), P(("row", "col"), None), P(), P(), P()),
        check_vma=False,
    )
```

```python
import jax
import jax.numpy as jnp
from jax import lax
from jax.experimental import pallas as pl
from jax.experimental.pallas import tpu as pltpu
from jax.sharding import PartitionSpec as P

MESH = pl.DeviceIdType.MESH
F32 = jnp.float32
BF16 = jnp.bfloat16
NZ, NY, NX = 8, 4, 4
NC = NY * NX
NR = 2 * NZ
T = 128
F = 256
SLOTS = 192
TILE_CUTS = 6
CUT = SLOTS // TILE_CUTS
PART = F // NC
HALF = T // 2
WPART = PART + 16
NT = (((1,), (1,)), ((), ()))
TN = (((0,), (0,)), ((), ()))


FIRST_LEG = (
    (2, 2, 0, 2, 1),
    (2, 1, 0, 1, 4),
    (2, 3, 0, 3, 3),
    (1, 2, 1, 0, 2),
    (3, 2, 3, 0, 0),
    (1, 1, 1, 1, 5),
    (1, 3, 1, 3, 6),
    (3, 1, 3, 1, 7),
    (3, 3, 3, 3, 8),
    (1, 0, 1, 0, 9),
    (3, 0, 3, 0, 10),
    (0, 1, 0, 1, 11),
    (0, 3, 0, 3, 12),
)
LINES = ((2, 0), (0, 2))
LINE_SLOTS = ((0, 1, 2), (3, 4))
OWN_WAYS = ((2, 0), (0, 2), (1, 0), (3, 0), (0, 1), (0, 3), (1, 1), (1, 3), (3, 1), (3, 3))
PASSED = (((0, 2), (0, 1), (0, 3)), ((1, 0), (3, 0)))
PAIRS = (
    ((0, 0), (2, 0)),
    ((0, 2), (1, 0)),
    ((3, 0), (0, 1)),
    ((0, 3), (1, 1)),
    ((1, 3), (3, 1)),
    ((3, 3), (2, 2)),
    ((2, 1), (2, 3)),
    ((1, 2), (3, 2)),
)
Z_ORDER = (4, 3, 5, 1, 7, 2, 6, 0)


def pick(i, values):
    if isinstance(i, int):
        return values[i]
    chosen = values[0]
    for n, value in enumerate(values[1:], 1):
        chosen = jnp.where(i == n, value, chosen)
    return chosen


def layer_kernel(
    feats, tiles, tile_row, tile_col, counts, w_self_h, w_neigh_h, bias, grad_out_h,
    out, d_feats, d_wself, d_wneigh, d_bias,
    w_self, w_neigh, grad_out, late_sem, tiles_v, run, tab_v, tab, a_ref, at_ref, acc, x_all, part, part_in, line_sum, line_in, degs, deg_in, pre_self, own_sum,
    back_all, sib_out, sib_in, comb, far_in, half_in, comb_in, grads, grads_in, w1_out, w1_in, w2_in, w3, w4_out, w4_in, self_grad,
    tile_sem, tab_sem, agz_s, agz_r, sib_s, sib_r, deg_s, deg_r, rs_s, rs_r, rl_s, rl_r, ag_s, ag_r, bs_s, bs_r, rz_s, rz_r,
    w0_s, w0_r, w1_s, w1_r, w2_s, w2_r, w3_s, w3_r, w4_s, w4_r,
):
    row = lax.axis_index("row")
    col = lax.axis_index("col")
    z, k = row // 2, row % 2
    y, x = col // NX, col % NX
    sibling = (z * 2 + (1 - k), col)

    def z_to(d):
        return (((z + d) % NZ) * 2 + k, col)

    def xy_index(p):
        return ((y + p // NX) % NY) * NX + (x + p % NX) % NX

    odd = (x + y) % 2

    def at(du, dv):
        yp = (y + (1 - odd) * du + odd * dv) % NY
        return yp * NX + (x + odd * du + (1 - odd) * dv) % NX

    def loop(lower, upper, body):
        def step(i, carry):
            body(i)
            return carry

        lax.fori_loop(lower, upper, step, 0)

    def remote(src, dst, send, recv, where):
        return pltpu.make_async_remote_copy(
            src_ref=src, dst_ref=dst, send_sem=send, recv_sem=recv, device_id=where, device_id_type=MESH
        )

    def tile_copy(i):
        cut = pl.ds(i * CUT, CUT)
        return pltpu.make_async_copy(tiles.at[cut], tiles_v.at[cut], tile_sem.at[i])

    for i in range(TILE_CUTS):
        tile_copy(i).start()

    late = [
        pltpu.make_async_copy(source, target, late_sem.at[i])
        for i, (source, target) in enumerate(((w_self_h, w_self), (w_neigh_h, w_neigh), (grad_out_h, grad_out)))
    ]
    for copy in late:
        copy.start()

    barrier = pltpu.get_barrier_semaphore()
    pl.semaphore_signal(barrier, inc=1, device_id=sibling, device_id_type=MESH)
    loop(1, NZ, lambda d: pl.semaphore_signal(barrier, inc=1, device_id=z_to(d), device_id_type=MESH))
    loop(1, NC, lambda p: pl.semaphore_signal(barrier, inc=1, device_id=(row, xy_index(p)), device_id_type=MESH))

    key_row = tile_row[...] * NR + tile_col[...]
    lane = lax.broadcasted_iota(jnp.int32, (1, SLOTS), 1)
    key_row = jnp.where(lane < counts[0], key_row, 4096)
    first = lax.broadcasted_iota(jnp.int32, (SLOTS, SLOTS), 0)
    second = lax.broadcasted_iota(jnp.int32, (SLOTS, SLOTS), 1)
    keys = jnp.broadcast_to(key_row, (SLOTS, SLOTS))
    key_col = jnp.sum(jnp.where(first == second, keys, 0), axis=1, keepdims=True)
    before = jnp.max(jnp.where((key_col == keys) & (first < second), first, -1), axis=0, keepdims=True)
    place = lax.broadcasted_iota(jnp.int32, (SLOTS, F), 1)
    slot = lax.broadcasted_iota(jnp.int32, (SLOTS, F), 0)
    last = jnp.max(jnp.where(key_col == place, slot, -1), axis=0, keepdims=True)
    tab_v[0:1, 0:SLOTS] = jnp.where(before < 0, SLOTS, before)
    tab_v[1:2, :] = jnp.where(last < 0, SLOTS, last)
    tab_copy = pltpu.make_async_copy(tab_v, tab, tab_sem)
    tab_copy.start()
    x_all[row] = feats[...]
    run[SLOTS] = jnp.zeros((T, T), F32)

    def add_up(s):
        for e in range(4):
            run[4 * s + e] = run[tab[0, 4 * s + e]] + tiles_v[4 * s + e].astype(F32)

    def add_cut(i):
        tile_copy(i).wait()
        loop(i * CUT // 4, (i + 1) * CUT // 4, add_up)

    tab_copy.wait()
    for i in range(2):
        add_cut(i)
    pl.semaphore_wait(barrier, 1 + (NZ - 1) + (NC - 1))

    def near(side):
        return remote(feats, x_all.at[row], agz_s.at[2 + side], agz_r.at[2 + side], z_to(NZ + 1 - 2 * side))

    def second(side, turn_in):
        half = pl.ds(HALF * (side + turn_in - 2 * side * turn_in), HALF)
        sem = 8 * turn_in + side
        return remote(
            feats.at[half], x_all.at[row, half], agz_s.at[sem], agz_r.at[sem], z_to(NZ + 2 * (1 - 2 * side))
        )

    def passed(side, turn_in):
        sign = 1 - 2 * side
        half = pl.ds(HALF * (side + turn_in - 2 * side * turn_in), HALF)
        block = x_all.at[((z + NZ - 2 * sign) % NZ) * 2 + k, half]
        sem = 4 + 6 * turn_in + side
        return remote(block, block, agz_s.at[sem], agz_r.at[sem], z_to(NZ + sign))

    def passed_half(side):
        sign = 1 - 2 * side
        block = x_all.at[((z + NZ - 2 * sign) % NZ) * 2 + k, pl.ds(side * HALF, HALF)]
        return remote(block, block, agz_s.at[6 + side], agz_r.at[6 + side], z_to(NZ + 2 * sign))

    for turn_in in range(2):
        for side in range(2):
            second(side, turn_in).start()
    for side in range(2):
        near(side).start()

    def to_sibling(zp):
        return remote(x_all.at[zp * 2 + k], x_all.at[zp * 2 + k], sib_s.at[zp], sib_r.at[zp], sibling)

    to_sibling(z).start()

    for i in range(2, TILE_CUTS):
        add_cut(i)

    def assemble(c):
        rows = pl.ds(pl.multiple_of(c * T, T), T)
        total = jnp.zeros((T, T), F32)
        for r in range(NR):
            block = run[tab[1, c * NR + r]]
            total = total + block
            a_ref[r // 2, rows, (r % 2) * T : (r % 2 + 1) * T] = block.astype(BF16)
        degs[c] = lax.dot_general(
            jnp.ones((8, T), F32), total, NT, preferred_element_type=F32, precision=lax.Precision.HIGHEST
        )

    loop(0, NC // 2, assemble)
    for side in range(2):
        second(side, 0).wait_recv()
        passed_half(side).start()
        passed(side, 0).start()
    for side in range(2):
        second(side, 1).wait_recv()
        passed(side, 1).start()
        to_sibling((z + NZ - 2 * (1 - 2 * side)) % NZ).start()
    loop(NC // 2, NC, assemble)

    def send_degree(p):
        return remote(degs.at[xy_index(p)], deg_in.at[p], deg_s.at[p], deg_r.at[p], (row, xy_index(p)))


    loop(1, NC, lambda p: send_degree(p).start())

    def multiply(left, right, add):
        term = jnp.dot(left, right, preferred_element_type=F32)
        acc[...] = acc[...] + term if add else term

    def pair_of(ref, i):
        return jnp.concatenate([ref[2 * i], ref[2 * i + 1]], axis=0)

    for side in range(2):
        near(side).wait_recv()
        to_sibling((z + NZ - (1 - 2 * side)) % NZ).start()
    to_sibling(z).wait_recv()
    multiply(a_ref[z], pair_of(x_all, z), False)

    def forward(i):
        zp = (z + pick(i, (6, 2, 7, 1, 5, 3))) % NZ
        to_sibling(zp).wait_recv()
        multiply(a_ref[zp], pair_of(x_all, zp), True)

    loop(0, 4, forward)
    for side in range(2):
        passed(side, 0).wait_recv()
        passed(side, 1).wait_recv()
        to_sibling((z + NZ - 3 * (1 - 2 * side)) % NZ).start()
    z_last = (z + NZ // 2) % NZ
    for side in range(2):
        block = x_all.at[z_last * 2 + k, pl.ds(side * HALF, HALF)]
        remote(block, block, agz_s.at[6 + side], agz_r.at[6 + side], sibling).wait_recv()
    to_sibling(z_last).start()
    loop(4, 6, forward)
    to_sibling(z_last).wait_recv()

    def send_part(du, dv, relay, slot, sem):
        return remote(part.at[at(du, dv)], part_in.at[slot], rs_s.at[sem], rs_r.at[slot], (row, at(*relay)))

    def took_part(slot):
        return remote(part_in.at[slot], part_in.at[slot], rs_s.at[0], rs_r.at[slot], sibling).wait_recv()

    x_last = pair_of(x_all, z_last)

    def finish(c):
        rows = pl.ds(pl.multiple_of(c * T, T), T)
        return acc[rows, :] + jnp.dot(a_ref[z_last, rows, :], x_last, preferred_element_type=F32)

    def part_copy(i):
        du, dv, ru, rv, slot = (pick(i, values) for values in zip(*FIRST_LEG))
        return du, dv, send_part(du, dv, (ru, rv), slot, i)

    def finish_send(i):
        du, dv, copy = part_copy(i)
        part[at(du, dv)] = finish(at(du, dv)).astype(BF16)
        copy.start()

    for i in range(len(FIRST_LEG)):
        finish_send(i)

    def finish_line(j):
        du, dv = LINES[j]
        own_rows = pl.ds(pl.multiple_of(at(du, dv) * T, T), T)
        acc[own_rows, :] = finish(at(du, dv))

    for j in range(2):
        finish_line(j)
    own_sum[...] = finish(col)


    def turn(c):
        rows = pl.ds(pl.multiple_of(c * T, T), T)
        for r in range(NR):
            at_ref[c, r * T : (r + 1) * T, :] = a_ref[r // 2, rows, (r % 2) * T : (r % 2 + 1) * T].T

    loop(0, NC // 2, turn)

    def send_line(j):
        return remote(line_sum.at[j], line_in.at[j], rl_s.at[j], rl_r.at[j], (row, at(*LINES[j])))

    def add_line(j):
        rows = pl.ds(pl.multiple_of(at(*LINES[j]) * T, T), T)
        total = acc[rows, :]
        for slot in LINE_SLOTS[j]:
            took_part(slot)
            total = total + part_in[slot].astype(F32)
        line_sum[j] = total.astype(BF16)
        send_line(j).start()

    for j in range(2):
        add_line(j)
    loop(NC // 2, NC, turn)
    for copy in late:
        copy.wait()
    pre_self[...] = jnp.dot(feats[...], w_self[...], preferred_element_type=F32) + bias[...]

    own_degree = degs[col]
    for p in range(1, NC):
        send_degree(p).wait_recv()
        own_degree = own_degree + deg_in[p]
    scale_row = lax.rsqrt(1.0 + own_degree[0:1, :])
    scale = jnp.broadcast_to(scale_row, (T, T)).T
    scale = jnp.concatenate([scale, scale], axis=1)

    def add_direct(slot):
        took_part(slot)
        own_sum[...] = own_sum[...] + part_in[slot].astype(F32)

    loop(5, 13, add_direct)
    for j in range(2):
        send_line(j).wait_recv()
        own_sum[...] = own_sum[...] + line_in[j].astype(F32)

    mixed = (own_sum[...] * scale).astype(BF16)
    pre = pre_self[...] + jnp.dot(mixed, w_neigh[...], preferred_element_type=F32)
    sig = 1.0 / (1.0 + jnp.exp(-pre))
    slope = sig * (1.0 + pre * (1.0 - sig))
    grad_pre = (grad_out[...].astype(F32) * slope).astype(BF16)
    back = lax.dot_general(grad_pre, w_neigh[...], NT, preferred_element_type=F32) * scale
    back_all[col] = back.astype(BF16)

    def send_back(source, du, dv, sem):
        return remote(back_all.at[source], back_all.at[source], ag_s.at[sem], ag_r.at[source], (row, at(du, dv)))

    def own_back(i):
        du, dv = (pick(i, values) for values in zip(*OWN_WAYS))
        return send_back(col, du, dv, i)

    def took_back(source):
        remote(back_all.at[source], back_all.at[source], ag_s.at[0], ag_r.at[source], sibling).wait_recv()

    def pass_back(f, e):
        return send_back(at(*LINES[f]), *PASSED[f][e], len(OWN_WAYS) + 3 * f + e)

    for i in range(6):
        own_back(i).start()
    out[...] = (pre * sig).astype(BF16)

    bias_sum = jnp.sum(grad_pre.astype(F32), axis=0, keepdims=True)
    grads[0, 0:F, :] = lax.dot_general(feats[...], grad_pre, TN, preferred_element_type=F32).astype(BF16)
    grads[1, 0:F, :] = lax.dot_general(mixed, grad_pre, TN, preferred_element_type=F32).astype(BF16)
    for i in range(2):
        grads[i, F : F + PART, :] = jnp.broadcast_to(bias_sum, (PART, F)).astype(BF16)
    w0 = remote(grads.at[1 - k], grads_in, w0_s, w0_r, sibling)
    w0.start()
    self_grad[...] = lax.dot_general(grad_pre, w_self[...], NT, preferred_element_type=F32)
    w0.wait_recv()
    bias_rows = slice(F, F + PART)
    bias_two = grads[k, bias_rows, :].astype(F32) + grads_in[bias_rows, :].astype(F32)

    def send_w1(p):
        return remote(w1_out.at[xy_index(p)], w1_in.at[p], w1_s.at[p], w1_r.at[p], (row, xy_index(p)))

    for c in range(NC):
        rows = slice(c * PART, (c + 1) * PART)
        w1_out[c] = (grads[k, rows, :].astype(F32) + grads_in[rows, :].astype(F32)).astype(BF16)
    loop(1, NC, lambda p: send_w1(p).start())
    for i in range(6, len(OWN_WAYS)):
        own_back(i).start()
    w2_in[z, PART:WPART, :] = bias_two.astype(BF16)

    for f in range(2):
        took_back(at(*LINES[f]))
        for e in range(len(PASSED[f])):
            pass_back(f, e).start()

    def pair_at(i):
        return tuple(at(*(pick(i, values) for values in zip(*(pair[n] for pair in PAIRS)))) for n in range(2))

    def two_of(ref, a, b, axis):
        return jnp.concatenate([ref[a], ref[b]], axis=axis)

    a, b = pair_at(0)
    multiply(two_of(at_ref, a, b, 1), two_of(back_all, a, b, 0), False)

    def backward(i):
        a, b = pair_at(i)
        pl.when(i > 1)(lambda: took_back(a))
        took_back(b)
        multiply(two_of(at_ref, a, b, 1), two_of(back_all, a, b, 0), True)

    loop(1, 3, backward)

    loop(1, NC, lambda p: send_w1(p).wait_recv())
    w1_sum = w1_out[col].astype(F32)
    for p in range(1, NC):
        w1_sum = w1_sum + w1_in[p].astype(F32)
    w2_in[z, 0:PART, :] = w1_sum.astype(BF16)

    def send_w2(d):
        return remote(w2_in.at[z], w2_in.at[z], w2_s.at[d], w2_r.at[d], z_to(d))

    loop(1, NZ, lambda d: send_w2(d).start())

    loop(3, 7, backward)
    b_first, b_second = pair_at(7)
    took_back(b_first)
    took_back(b_second)
    b_last = two_of(back_all, b_first, b_second, 0)

    def finish_back(r):
        rows = pl.ds(pl.multiple_of(r * T, T), T)
        left = jnp.concatenate([at_ref[b_first, rows, :], at_ref[b_second, rows, :]], axis=1)
        return acc[rows, :] + jnp.dot(left, b_last, preferred_element_type=F32)

    def to_sibling_back(zp):
        return remote(sib_out.at[zp], sib_in.at[zp], bs_s.at[zp], bs_r.at[zp], sibling)

    def give_sibling(i):
        zp = (z + pick(i, Z_ORDER)) % NZ
        sib_out[zp] = finish_back(zp * 2 + 1 - k).astype(BF16)
        to_sibling_back(zp).start()

    for i in range(NZ):
        give_sibling(i)

    def combine(zp):
        to_sibling_back(zp).wait_recv()
        return finish_back(zp * 2 + k) + sib_in[zp].astype(F32)

    def send_half(side):
        sign = 1 - 2 * side
        half = comb.at[(z + NZ // 2) % NZ, pl.ds(side * HALF, HALF)]
        return remote(half, half_in.at[side], rz_s.at[side], rz_r.at[side], z_to(NZ - 2 * sign))

    def send_far(side):
        sign = 1 - 2 * side
        block = comb.at[(z + NZ - 3 * sign) % NZ]
        return remote(block, far_in.at[side], rz_s.at[2 + side], rz_r.at[2 + side], z_to(NZ - sign))

    def send_comb(side, hops):
        sign = 1 - 2 * side
        slot = 2 * (hops - 1) + side
        block = comb.at[(z + NZ - hops * sign) % NZ]
        return remote(block, comb_in.at[slot], rz_s.at[4 + slot], rz_r.at[4 + slot], z_to(NZ - hops * sign))

    z_four = (z + NZ // 2) % NZ
    comb[z_four] = combine(z_four).astype(BF16)
    for side in range(2):
        send_half(side).start()
    for side in range(2):
        zp = (z + NZ - 3 * (1 - 2 * side)) % NZ
        comb[zp] = combine(zp).astype(BF16)
        send_far(side).start()
    for side in range(2):
        zp = (z + NZ - (1 - 2 * side)) % NZ
        comb[zp] = combine(zp).astype(BF16)
        send_comb(side, 1).start()
    own_sum[...] = combine(z) + self_grad[...]

    loop(1, NZ, lambda d: send_w2(d).wait_recv())
    w2_sum = w2_in[0].astype(F32)
    for zp in range(1, NZ):
        w2_sum = w2_sum + w2_in[zp].astype(F32)
    w3[col] = w2_sum.astype(BF16)

    def send_w3(p):
        return remote(w3.at[col], w3.at[col], w3_s.at[p], w3_r.at[p], (row, xy_index(p)))

    loop(1, NC, lambda p: send_w3(p).start())

    for side in range(2):
        zp = (z + NZ - 2 * (1 - 2 * side)) % NZ
        total = combine(zp)
        send_far(side).wait_recv()
        total = total + far_in[side].astype(F32)
        send_half(side).wait_recv()
        added = half_in[side].astype(F32)
        zeros = jnp.zeros((HALF, F), F32)
        total = total + jnp.concatenate([zeros, added] if side else [added, zeros], axis=0)
        comb[zp] = total.astype(BF16)
        send_comb(side, 2).start()

    loop(1, NC, lambda p: send_w3(p).wait_recv())
    bias_all = w3[0, PART : PART + 1, :].astype(F32)
    for c in range(1, NC):
        bias_all = bias_all + w3[c, PART : PART + 1, :].astype(F32)
    d_bias[...] = bias_all
    for c in range(NC):
        w4_out[c * PART : (c + 1) * PART, :] = w3[c, 0:PART, :]
    w4 = remote(w4_out, w4_in, w4_s, w4_r, sibling)
    w4.start()

    for hops in (1, 2):
        for side in range(2):
            send_comb(side, hops).wait_recv()
            own_sum[...] = own_sum[...] + comb_in[2 * (hops - 1) + side].astype(F32)
    d_feats[...] = own_sum[...].astype(BF16)

    w4.wait_recv()
    core = jnp.full((F, F), k, jnp.int32)
    mine = w4_out[...]
    other = w4_in[...]
    d_wself[...] = jnp.where(core == 0, mine, other)
    d_wneigh[...] = jnp.where(core == 0, other, mine)

    for side in range(2):
        near(side).wait_send()
        for turn_in in range(2):
            second(side, turn_in).wait_send()
            passed(side, turn_in).wait_send()
        passed_half(side).wait_send()
        send_half(side).wait_send()
        send_far(side).wait_send()
        send_comb(side, 1).wait_send()
        send_comb(side, 2).wait_send()

    def sent_z(d):
        send_w2(d).wait_send()

    loop(1, NZ, sent_z)

    def sent_xy(p):
        send_degree(p).wait_send()
        send_w1(p).wait_send()
        send_w3(p).wait_send()

    loop(1, NC, sent_xy)
    loop(0, len(FIRST_LEG), lambda i: part_copy(i)[2].wait_send())
    for j in range(2):
        send_line(j).wait_send()
    loop(0, len(OWN_WAYS), lambda i: own_back(i).wait_send())
    for f in range(2):
        for e in range(len(PASSED[f])):
            pass_back(f, e).wait_send()

    def sent_sibling(zp):
        to_sibling(zp).wait_send()
        to_sibling_back(zp).wait_send()

    loop(0, NZ, sent_sibling)
    w0.wait_send()
    w4.wait_send()


def hand_over(*refs):
    for source, target in zip(refs[:5], refs[5:]):
        target[...] = source[...].astype(target.dtype)


def per_device(feats, tiles, tile_row, tile_col, counts, w_self, w_neigh, bias, grad_out):
    vmem = pl.BlockSpec(memory_space=pltpu.VMEM)
    dma = pltpu.SemaphoreType.DMA
    outs = pl.pallas_call(
        layer_kernel,
        out_shape=(
            jax.ShapeDtypeStruct((T, F), BF16),
            jax.ShapeDtypeStruct((T, F), BF16),
            jax.ShapeDtypeStruct((F, F), BF16),
            jax.ShapeDtypeStruct((F, F), BF16),
            jax.ShapeDtypeStruct((1, F), F32),
        ),
        in_specs=[
            vmem,
            pl.BlockSpec(memory_space=pl.ANY),
            vmem,
            vmem,
            pl.BlockSpec(memory_space=pltpu.SMEM),
            pl.BlockSpec(memory_space=pl.ANY),
            pl.BlockSpec(memory_space=pl.ANY),
            vmem,
            pl.BlockSpec(memory_space=pl.ANY),
        ],
        out_specs=(vmem,) * 5,
        scratch_shapes=[
            pltpu.VMEM((F, F), BF16),
            pltpu.VMEM((F, F), BF16),
            pltpu.VMEM((T, F), BF16),
            dma((3,)),
            pltpu.VMEM((SLOTS, T, T), BF16),
            pltpu.VMEM((SLOTS + 1, T, T), F32),
            pltpu.VMEM((8, F), jnp.int32),
            pltpu.SMEM((8, F), jnp.int32),
            pltpu.VMEM((NZ, NC * T, 2 * T), BF16),
            pltpu.VMEM((NC, NR * T, T), BF16),
            pltpu.VMEM((NC * T, F), F32),
            pltpu.VMEM((NR, T, F), BF16),
            pltpu.VMEM((NC, T, F), BF16),
            pltpu.VMEM((NC, T, F), BF16),
            pltpu.VMEM((2, T, F), BF16),
            pltpu.VMEM((2, T, F), BF16),
            pltpu.VMEM((NC, 8, T), F32),
            pltpu.VMEM((NC, 8, T), F32),
            pltpu.VMEM((T, F), F32),
            pltpu.VMEM((T, F), F32),
            pltpu.VMEM((NC, T, F), BF16),
            pltpu.VMEM((NZ, T, F), BF16),
            pltpu.VMEM((NZ, T, F), BF16),
            pltpu.VMEM((NZ, T, F), BF16),
            pltpu.VMEM((2, T, F), BF16),
            pltpu.VMEM((2, HALF, F), BF16),
            pltpu.VMEM((4, T, F), BF16),
            pltpu.VMEM((2, F + PART, F), BF16),
            pltpu.VMEM((F + PART, F), BF16),
            pltpu.VMEM((NC, PART, F), BF16),
            pltpu.VMEM((NC, PART, F), BF16),
            pltpu.VMEM((NZ, WPART, F), BF16),
            pltpu.VMEM((NC, WPART, F), BF16),
            pltpu.VMEM((F, F), BF16),
            pltpu.VMEM((F, F), BF16),
            pltpu.VMEM((T, F), F32),
            dma((TILE_CUTS,)),
            dma,
        ]
        + [dma((NZ + 4,))] * 2
        + [dma((NZ,))] * 2
        + [dma((NC,))] * 4
        + [dma((2,))] * 2
        + [dma((NC,))] * 2
        + [dma((NZ,))] * 4
        + [dma, dma]
        + [dma((NC,))] * 2
        + [dma((NZ,))] * 2
        + [dma((NC,))] * 2
        + [dma, dma],
        compiler_params=pltpu.CompilerParams(
            collective_id=0, has_side_effects=True, vmem_limit_bytes=56 * 2**20
        ),
        name="sage_layer",
    )(
        feats,
        tiles.reshape(SLOTS, T, T),
        tile_row,
        tile_col,
        counts,
        w_self,
        w_neigh,
        bias.reshape(1, F),
        grad_out,
    )
    outs = pl.pallas_call(
        hand_over,
        out_shape=[jax.ShapeDtypeStruct(o.shape, t) for o, t in zip(outs, (BF16, BF16, F32, F32, F32))],
        in_specs=[vmem] * 5,
        out_specs=[vmem] * 5,
        name="hand_over",
    )(*outs)
    return (outs[0], outs[1], outs[2], outs[3], outs[4].reshape(F))


def solution(mesh):
    placed = (
        P(("row", "col"), None),
        P(("row", "col"), None, None, None),
        P(("row", "col"), None),
        P(("row", "col"), None),
        P(("row", "col")),
        P(),
        P(),
        P(),
        P(("row", "col"), None),
    )
    return jax.shard_map(
        per_device,
        mesh=mesh,
        in_specs=placed,
        out_specs=(P(("row", "col"), None), P(("row", "col"), None), P(), P(), P()),
        check_vma=False,
    )
```

```python
import jax
import jax.numpy as jnp
from jax import lax
from jax.experimental import pallas as pl
from jax.experimental.pallas import tpu as pltpu
from jax.sharding import PartitionSpec as P

MESH = pl.DeviceIdType.MESH
F32 = jnp.float32
BF16 = jnp.bfloat16
NZ, NY, NX = 8, 4, 4
NC = NY * NX
NR = 2 * NZ
T = 128
F = 256
SLOTS = 192
TILE_CUTS = 6
CUT = SLOTS // TILE_CUTS
PART = F // NC
HALF = T // 2
WPART = PART + 16
NT = (((1,), (1,)), ((), ()))
TN = (((0,), (0,)), ((), ()))


FIRST_LEG = (
    (2, 2, 0, 2, 1),
    (2, 1, 0, 1, 4),
    (2, 3, 0, 3, 3),
    (1, 2, 1, 0, 2),
    (3, 2, 3, 0, 0),
    (1, 1, 1, 1, 5),
    (1, 3, 1, 3, 6),
    (3, 1, 3, 1, 7),
    (3, 3, 3, 3, 8),
    (1, 0, 1, 0, 9),
    (3, 0, 3, 0, 10),
    (0, 1, 0, 1, 11),
    (0, 3, 0, 3, 12),
)
LINES = ((2, 0), (0, 2))
LINE_SLOTS = ((0, 1, 2), (3, 4))
OWN_WAYS = ((2, 0), (0, 2), (1, 0), (3, 0), (0, 1), (0, 3), (1, 1), (1, 3), (3, 1), (3, 3))
PASSED = (((0, 2), (0, 1), (0, 3)), ((1, 0), (3, 0)))
PAIRS = (
    ((0, 0), (2, 0)),
    ((0, 2), (1, 0)),
    ((3, 0), (0, 1)),
    ((0, 3), (1, 1)),
    ((1, 3), (3, 1)),
    ((3, 3), (2, 2)),
    ((2, 1), (2, 3)),
    ((1, 2), (3, 2)),
)
Z_ORDER = (4, 3, 5, 1, 7, 2, 6, 0)


def pick(i, values):
    if isinstance(i, int):
        return values[i]
    chosen = values[0]
    for n, value in enumerate(values[1:], 1):
        chosen = jnp.where(i == n, value, chosen)
    return chosen


def layer_kernel(
    feats, tiles, tile_row, tile_col, counts, w_self_h, w_neigh_h, bias, grad_out_h,
    out, d_feats, d_wself, d_wneigh, d_bias,
    w_self, w_neigh, grad_out, late_sem, tiles_v, run, tab_v, tab, a_ref, at_ref, acc, x_all, part, part_in, line_sum, line_in, degs, deg_in, pre_self, own_sum,
    back_all, sib_out, sib_in, comb, far_in, half_in, comb_in, grads, grads_in, w1_out, w1_in, w2_in, w3, w4_out, w4_in, self_grad,
    tile_sem, tab_sem, agz_s, agz_r, sib_s, sib_r, deg_s, deg_r, rs_s, rs_r, rl_s, rl_r, ag_s, ag_r, bs_s, bs_r, rz_s, rz_r,
    w0_s, w0_r, w1_s, w1_r, w2_s, w2_r, w3_s, w3_r, w4_s, w4_r,
):
    row = lax.axis_index("row")
    col = lax.axis_index("col")
    z, k = row // 2, row % 2
    y, x = col // NX, col % NX
    sibling = (z * 2 + (1 - k), col)

    def z_to(d):
        return (((z + d) % NZ) * 2 + k, col)

    def xy_index(p):
        return ((y + p // NX) % NY) * NX + (x + p % NX) % NX

    odd = (x + y) % 2

    def at(du, dv):
        yp = (y + (1 - odd) * du + odd * dv) % NY
        return yp * NX + (x + odd * du + (1 - odd) * dv) % NX

    def loop(lower, upper, body):
        def step(i, carry):
            body(i)
            return carry

        lax.fori_loop(lower, upper, step, 0)

    def remote(src, dst, send, recv, where):
        return pltpu.make_async_remote_copy(
            src_ref=src, dst_ref=dst, send_sem=send, recv_sem=recv, device_id=where, device_id_type=MESH
        )

    def tile_copy(i):
        cut = pl.ds(i * CUT, CUT)
        return pltpu.make_async_copy(tiles.at[cut], tiles_v.at[cut], tile_sem.at[i])

    for i in range(TILE_CUTS):
        tile_copy(i).start()

    late = [
        pltpu.make_async_copy(source, target, late_sem.at[i])
        for i, (source, target) in enumerate(((w_self_h, w_self), (w_neigh_h, w_neigh), (grad_out_h, grad_out)))
    ]
    for copy in late:
        copy.start()

    barrier = pltpu.get_barrier_semaphore()
    pl.semaphore_signal(barrier, inc=1, device_id=sibling, device_id_type=MESH)
    loop(1, NZ, lambda d: pl.semaphore_signal(barrier, inc=1, device_id=z_to(d), device_id_type=MESH))
    loop(1, NC, lambda p: pl.semaphore_signal(barrier, inc=1, device_id=(row, xy_index(p)), device_id_type=MESH))

    key_row = tile_row[...] * NR + tile_col[...]
    lane = lax.broadcasted_iota(jnp.int32, (1, SLOTS), 1)
    key_row = jnp.where(lane < counts[0], key_row, 4096)
    first = lax.broadcasted_iota(jnp.int32, (SLOTS, SLOTS), 0)
    second = lax.broadcasted_iota(jnp.int32, (SLOTS, SLOTS), 1)
    keys = jnp.broadcast_to(key_row, (SLOTS, SLOTS))
    key_col = jnp.sum(jnp.where(first == second, keys, 0), axis=1, keepdims=True)
    before = jnp.max(jnp.where((key_col == keys) & (first < second), first, -1), axis=0, keepdims=True)
    place = lax.broadcasted_iota(jnp.int32, (SLOTS, F), 1)
    slot = lax.broadcasted_iota(jnp.int32, (SLOTS, F), 0)
    last = jnp.max(jnp.where(key_col == place, slot, -1), axis=0, keepdims=True)
    tab_v[0:1, 0:SLOTS] = jnp.where(before < 0, SLOTS, before)
    tab_v[1:2, :] = jnp.where(last < 0, SLOTS, last)
    tab_copy = pltpu.make_async_copy(tab_v, tab, tab_sem)
    tab_copy.start()
    x_all[row] = feats[...]
    run[SLOTS] = jnp.zeros((T, T), F32)

    def add_up(s):
        for e in range(4):
            run[4 * s + e] = run[tab[0, 4 * s + e]] + tiles_v[4 * s + e].astype(F32)

    def add_cut(i):
        tile_copy(i).wait()
        loop(i * CUT // 4, (i + 1) * CUT // 4, add_up)

    tab_copy.wait()
    for i in range(2):
        add_cut(i)
    pl.semaphore_wait(barrier, 1 + (NZ - 1) + (NC - 1))

    def near(side):
        return remote(feats, x_all.at[row], agz_s.at[2 + side], agz_r.at[2 + side], z_to(NZ + 1 - 2 * side))

    def second(side, turn_in):
        half = pl.ds(HALF * (side + turn_in - 2 * side * turn_in), HALF)
        sem = 8 * turn_in + side
        return remote(
            feats.at[half], x_all.at[row, half], agz_s.at[sem], agz_r.at[sem], z_to(NZ + 2 * (1 - 2 * side))
        )

    def passed(side, turn_in):
        sign = 1 - 2 * side
        half = pl.ds(HALF * (side + turn_in - 2 * side * turn_in), HALF)
        block = x_all.at[((z + NZ - 2 * sign) % NZ) * 2 + k, half]
        sem = 4 + 6 * turn_in + side
        return remote(block, block, agz_s.at[sem], agz_r.at[sem], z_to(NZ + sign))

    def passed_half(side):
        sign = 1 - 2 * side
        block = x_all.at[((z + NZ - 2 * sign) % NZ) * 2 + k, pl.ds(side * HALF, HALF)]
        return remote(block, block, agz_s.at[6 + side], agz_r.at[6 + side], z_to(NZ + 2 * sign))

    for turn_in in range(2):
        for side in range(2):
            second(side, turn_in).start()
    for side in range(2):
        near(side).start()

    def to_sibling(zp):
        return remote(x_all.at[zp * 2 + k], x_all.at[zp * 2 + k], sib_s.at[zp], sib_r.at[zp], sibling)

    to_sibling(z).start()

    for i in range(2, TILE_CUTS):
        add_cut(i)

    def assemble(c):
        rows = pl.ds(pl.multiple_of(c * T, T), T)
        total = jnp.zeros((T, T), F32)
        for r in range(NR):
            block = run[tab[1, c * NR + r]]
            total = total + block
            a_ref[r // 2, rows, (r % 2) * T : (r % 2 + 1) * T] = block.astype(BF16)
        degs[c] = lax.dot_general(
            jnp.ones((8, T), F32), total, NT, preferred_element_type=F32, precision=lax.Precision.HIGHEST
        )

    loop(0, NC // 2, assemble)
    for side in range(2):
        second(side, 0).wait_recv()
        passed_half(side).start()
        passed(side, 0).start()
    for side in range(2):
        second(side, 1).wait_recv()
        passed(side, 1).start()
        to_sibling((z + NZ - 2 * (1 - 2 * side)) % NZ).start()
    loop(NC // 2, NC, assemble)

    def send_degree(p):
        return remote(degs.at[xy_index(p)], deg_in.at[p], deg_s.at[p], deg_r.at[p], (row, xy_index(p)))


    loop(1, NC, lambda p: send_degree(p).start())

    def multiply(left, right, add):
        term = jnp.dot(left, right, preferred_element_type=F32)
        acc[...] = acc[...] + term if add else term

    def pair_of(ref, i):
        return jnp.concatenate([ref[2 * i], ref[2 * i + 1]], axis=0)

    for side in range(2):
        near(side).wait_recv()
        to_sibling((z + NZ - (1 - 2 * side)) % NZ).start()
    to_sibling(z).wait_recv()
    multiply(a_ref[z], pair_of(x_all, z), False)

    def forward(i):
        zp = (z + pick(i, (6, 2, 7, 1, 5, 3))) % NZ
        to_sibling(zp).wait_recv()
        multiply(a_ref[zp], pair_of(x_all, zp), True)

    loop(0, 4, forward)
    for side in range(2):
        passed(side, 0).wait_recv()
        passed(side, 1).wait_recv()
        to_sibling((z + NZ - 3 * (1 - 2 * side)) % NZ).start()
    z_last = (z + NZ // 2) % NZ
    for side in range(2):
        block = x_all.at[z_last * 2 + k, pl.ds(side * HALF, HALF)]
        remote(block, block, agz_s.at[6 + side], agz_r.at[6 + side], sibling).wait_recv()
    to_sibling(z_last).start()
    loop(4, 6, forward)
    to_sibling(z_last).wait_recv()

    def send_part(du, dv, relay, slot, sem):
        return remote(part.at[at(du, dv)], part_in.at[slot], rs_s.at[sem], rs_r.at[slot], (row, at(*relay)))

    def took_part(slot):
        return remote(part_in.at[slot], part_in.at[slot], rs_s.at[0], rs_r.at[slot], sibling).wait_recv()

    x_last = pair_of(x_all, z_last)

    def finish(c):
        rows = pl.ds(pl.multiple_of(c * T, T), T)
        return acc[rows, :] + jnp.dot(a_ref[z_last, rows, :], x_last, preferred_element_type=F32)

    def part_copy(i):
        du, dv, ru, rv, slot = (pick(i, values) for values in zip(*FIRST_LEG))
        return du, dv, send_part(du, dv, (ru, rv), slot, i)

    def finish_send(i):
        du, dv, copy = part_copy(i)
        part[at(du, dv)] = finish(at(du, dv)).astype(BF16)
        copy.start()

    for i in range(len(FIRST_LEG)):
        finish_send(i)

    def finish_line(j):
        du, dv = LINES[j]
        own_rows = pl.ds(pl.multiple_of(at(du, dv) * T, T), T)
        acc[own_rows, :] = finish(at(du, dv))

    for j in range(2):
        finish_line(j)
    own_sum[...] = finish(col)


    def turn(c):
        rows = pl.ds(pl.multiple_of(c * T, T), T)
        for r in range(NR):
            at_ref[c, r * T : (r + 1) * T, :] = a_ref[r // 2, rows, (r % 2) * T : (r % 2 + 1) * T].T

    loop(0, NC // 2, turn)

    def send_line(j):
        return remote(line_sum.at[j], line_in.at[j], rl_s.at[j], rl_r.at[j], (row, at(*LINES[j])))

    def add_line(j):
        rows = pl.ds(pl.multiple_of(at(*LINES[j]) * T, T), T)
        total = acc[rows, :]
        for slot in LINE_SLOTS[j]:
            took_part(slot)
            total = total + part_in[slot].astype(F32)
        line_sum[j] = total.astype(BF16)
        send_line(j).start()

    for j in range(2):
        add_line(j)
    loop(NC // 2, NC, turn)
    for copy in late:
        copy.wait()
    pre_self[...] = jnp.dot(feats[...], w_self[...], preferred_element_type=F32) + bias[...]

    own_degree = degs[col]
    for p in range(1, NC):
        send_degree(p).wait_recv()
        own_degree = own_degree + deg_in[p]
    scale_row = lax.rsqrt(1.0 + own_degree[0:1, :])
    scale = jnp.broadcast_to(scale_row, (T, T)).T
    scale = jnp.concatenate([scale, scale], axis=1)

    def add_direct(slot):
        took_part(slot)
        own_sum[...] = own_sum[...] + part_in[slot].astype(F32)

    loop(5, 13, add_direct)
    for j in range(2):
        send_line(j).wait_recv()
        own_sum[...] = own_sum[...] + line_in[j].astype(F32)

    mixed = (own_sum[...] * scale).astype(BF16)
    pre = pre_self[...] + jnp.dot(mixed, w_neigh[...], preferred_element_type=F32)
    sig = 1.0 / (1.0 + jnp.exp(-pre))
    slope = sig * (1.0 + pre * (1.0 - sig))
    grad_pre = (grad_out[...].astype(F32) * slope).astype(BF16)
    back = lax.dot_general(grad_pre, w_neigh[...], NT, preferred_element_type=F32) * scale
    back_all[col] = back.astype(BF16)

    def send_back(source, du, dv, sem):
        return remote(back_all.at[source], back_all.at[source], ag_s.at[sem], ag_r.at[source], (row, at(du, dv)))

    def own_back(i):
        du, dv = (pick(i, values) for values in zip(*OWN_WAYS))
        return send_back(col, du, dv, i)

    def took_back(source):
        remote(back_all.at[source], back_all.at[source], ag_s.at[0], ag_r.at[source], sibling).wait_recv()

    def pass_back(f, e):
        return send_back(at(*LINES[f]), *PASSED[f][e], len(OWN_WAYS) + 3 * f + e)

    for i in range(6):
        own_back(i).start()
    out[...] = (pre * sig).astype(BF16)

    bias_sum = jnp.sum(grad_pre.astype(F32), axis=0, keepdims=True)
    grads[0, 0:F, :] = lax.dot_general(feats[...], grad_pre, TN, preferred_element_type=F32).astype(BF16)
    grads[1, 0:F, :] = lax.dot_general(mixed, grad_pre, TN, preferred_element_type=F32).astype(BF16)
    for i in range(2):
        grads[i, F : F + PART, :] = jnp.broadcast_to(bias_sum, (PART, F)).astype(BF16)
    w0 = remote(grads.at[1 - k], grads_in, w0_s, w0_r, sibling)
    w0.start()
    self_grad[...] = lax.dot_general(grad_pre, w_self[...], NT, preferred_element_type=F32)
    w0.wait_recv()
    bias_rows = slice(F, F + PART)
    bias_two = grads[k, bias_rows, :].astype(F32) + grads_in[bias_rows, :].astype(F32)

    def send_w1(p):
        return remote(w1_out.at[xy_index(p)], w1_in.at[p], w1_s.at[p], w1_r.at[p], (row, xy_index(p)))

    for c in range(NC):
        rows = slice(c * PART, (c + 1) * PART)
        w1_out[c] = (grads[k, rows, :].astype(F32) + grads_in[rows, :].astype(F32)).astype(BF16)
    for p in range(1, NC):
        send_w1(p).start()
    for i in range(6, len(OWN_WAYS)):
        own_back(i).start()
    w2_in[z, PART:WPART, :] = bias_two.astype(BF16)

    for f in range(2):
        took_back(at(*LINES[f]))
        for e in range(len(PASSED[f])):
            pass_back(f, e).start()

    def pair_at(i):
        return tuple(at(*(pick(i, values) for values in zip(*(pair[n] for pair in PAIRS)))) for n in range(2))

    def two_of(ref, a, b, axis):
        return jnp.concatenate([ref[a], ref[b]], axis=axis)

    a, b = pair_at(0)
    multiply(two_of(at_ref, a, b, 1), two_of(back_all, a, b, 0), False)

    def backward(i):
        a, b = pair_at(i)
        pl.when(i > 1)(lambda: took_back(a))
        took_back(b)
        multiply(two_of(at_ref, a, b, 1), two_of(back_all, a, b, 0), True)

    loop(1, 3, backward)

    loop(1, NC, lambda p: send_w1(p).wait_recv())
    w1_sum = w1_out[col].astype(F32)
    for p in range(1, NC):
        w1_sum = w1_sum + w1_in[p].astype(F32)
    w2_in[z, 0:PART, :] = w1_sum.astype(BF16)

    def send_w2(d):
        return remote(w2_in.at[z], w2_in.at[z], w2_s.at[d], w2_r.at[d], z_to(d))

    for d in range(1, NZ):
        send_w2(d).start()

    loop(3, 7, backward)
    b_first, b_second = pair_at(7)
    took_back(b_first)
    took_back(b_second)
    b_last = two_of(back_all, b_first, b_second, 0)

    def finish_back(r):
        rows = pl.ds(pl.multiple_of(r * T, T), T)
        left = jnp.concatenate([at_ref[b_first, rows, :], at_ref[b_second, rows, :]], axis=1)
        return acc[rows, :] + jnp.dot(left, b_last, preferred_element_type=F32)

    def to_sibling_back(zp):
        return remote(sib_out.at[zp], sib_in.at[zp], bs_s.at[zp], bs_r.at[zp], sibling)

    def give_sibling(i):
        zp = (z + pick(i, Z_ORDER)) % NZ
        sib_out[zp] = finish_back(zp * 2 + 1 - k).astype(BF16)
        to_sibling_back(zp).start()

    for i in range(NZ):
        give_sibling(i)

    def combine(zp):
        to_sibling_back(zp).wait_recv()
        return finish_back(zp * 2 + k) + sib_in[zp].astype(F32)

    def send_half(side):
        sign = 1 - 2 * side
        half = comb.at[(z + NZ // 2) % NZ, pl.ds(side * HALF, HALF)]
        return remote(half, half_in.at[side], rz_s.at[side], rz_r.at[side], z_to(NZ - 2 * sign))

    def send_far(side):
        sign = 1 - 2 * side
        block = comb.at[(z + NZ - 3 * sign) % NZ]
        return remote(block, far_in.at[side], rz_s.at[2 + side], rz_r.at[2 + side], z_to(NZ - sign))

    def send_comb(side, hops):
        sign = 1 - 2 * side
        slot = 2 * (hops - 1) + side
        block = comb.at[(z + NZ - hops * sign) % NZ]
        return remote(block, comb_in.at[slot], rz_s.at[4 + slot], rz_r.at[4 + slot], z_to(NZ - hops * sign))

    z_four = (z + NZ // 2) % NZ
    comb[z_four] = combine(z_four).astype(BF16)
    for side in range(2):
        send_half(side).start()
    for side in range(2):
        zp = (z + NZ - 3 * (1 - 2 * side)) % NZ
        comb[zp] = combine(zp).astype(BF16)
        send_far(side).start()
    for side in range(2):
        zp = (z + NZ - (1 - 2 * side)) % NZ
        comb[zp] = combine(zp).astype(BF16)
        send_comb(side, 1).start()
    own_sum[...] = combine(z) + self_grad[...]

    loop(1, NZ, lambda d: send_w2(d).wait_recv())
    w2_sum = w2_in[0].astype(F32)
    for zp in range(1, NZ):
        w2_sum = w2_sum + w2_in[zp].astype(F32)
    w3[col] = w2_sum.astype(BF16)

    def send_w3(p):
        return remote(w3.at[col], w3.at[col], w3_s.at[p], w3_r.at[p], (row, xy_index(p)))

    for p in range(1, NC):
        send_w3(p).start()

    for side in range(2):
        zp = (z + NZ - 2 * (1 - 2 * side)) % NZ
        total = combine(zp)
        send_far(side).wait_recv()
        total = total + far_in[side].astype(F32)
        send_half(side).wait_recv()
        added = half_in[side].astype(F32)
        zeros = jnp.zeros((HALF, F), F32)
        total = total + jnp.concatenate([zeros, added] if side else [added, zeros], axis=0)
        comb[zp] = total.astype(BF16)
        send_comb(side, 2).start()

    loop(1, NC, lambda p: send_w3(p).wait_recv())
    bias_all = w3[0, PART : PART + 1, :].astype(F32)
    for c in range(1, NC):
        bias_all = bias_all + w3[c, PART : PART + 1, :].astype(F32)
    d_bias[...] = bias_all
    for c in range(NC):
        w4_out[c * PART : (c + 1) * PART, :] = w3[c, 0:PART, :]
    w4 = remote(w4_out, w4_in, w4_s, w4_r, sibling)
    w4.start()

    for hops in (1, 2):
        for side in range(2):
            send_comb(side, hops).wait_recv()
            own_sum[...] = own_sum[...] + comb_in[2 * (hops - 1) + side].astype(F32)
    d_feats[...] = own_sum[...].astype(BF16)

    w4.wait_recv()
    core = jnp.full((F, F), k, jnp.int32)
    mine = w4_out[...]
    other = w4_in[...]
    d_wself[...] = jnp.where(core == 0, mine, other)
    d_wneigh[...] = jnp.where(core == 0, other, mine)

    for side in range(2):
        near(side).wait_send()
        for turn_in in range(2):
            second(side, turn_in).wait_send()
            passed(side, turn_in).wait_send()
        passed_half(side).wait_send()
        send_half(side).wait_send()
        send_far(side).wait_send()
        send_comb(side, 1).wait_send()
        send_comb(side, 2).wait_send()

    def sent_z(d):
        send_w2(d).wait_send()

    loop(1, NZ, sent_z)

    def sent_xy(p):
        send_degree(p).wait_send()
        send_w1(p).wait_send()
        send_w3(p).wait_send()

    loop(1, NC, sent_xy)
    loop(0, len(FIRST_LEG), lambda i: part_copy(i)[2].wait_send())
    for j in range(2):
        send_line(j).wait_send()
    loop(0, len(OWN_WAYS), lambda i: own_back(i).wait_send())
    for f in range(2):
        for e in range(len(PASSED[f])):
            pass_back(f, e).wait_send()

    def sent_sibling(zp):
        to_sibling(zp).wait_send()
        to_sibling_back(zp).wait_send()

    loop(0, NZ, sent_sibling)
    w0.wait_send()
    w4.wait_send()


def hand_over(*refs):
    for source, target in zip(refs[:5], refs[5:]):
        target[...] = source[...].astype(target.dtype)


def per_device(feats, tiles, tile_row, tile_col, counts, w_self, w_neigh, bias, grad_out):
    vmem = pl.BlockSpec(memory_space=pltpu.VMEM)
    dma = pltpu.SemaphoreType.DMA
    outs = pl.pallas_call(
        layer_kernel,
        out_shape=(
            jax.ShapeDtypeStruct((T, F), BF16),
            jax.ShapeDtypeStruct((T, F), BF16),
            jax.ShapeDtypeStruct((F, F), BF16),
            jax.ShapeDtypeStruct((F, F), BF16),
            jax.ShapeDtypeStruct((1, F), F32),
        ),
        in_specs=[
            vmem,
            pl.BlockSpec(memory_space=pl.ANY),
            vmem,
            vmem,
            pl.BlockSpec(memory_space=pltpu.SMEM),
            pl.BlockSpec(memory_space=pl.ANY),
            pl.BlockSpec(memory_space=pl.ANY),
            vmem,
            pl.BlockSpec(memory_space=pl.ANY),
        ],
        out_specs=(vmem,) * 5,
        scratch_shapes=[
            pltpu.VMEM((F, F), BF16),
            pltpu.VMEM((F, F), BF16),
            pltpu.VMEM((T, F), BF16),
            dma((3,)),
            pltpu.VMEM((SLOTS, T, T), BF16),
            pltpu.VMEM((SLOTS + 1, T, T), F32),
            pltpu.VMEM((8, F), jnp.int32),
            pltpu.SMEM((8, F), jnp.int32),
            pltpu.VMEM((NZ, NC * T, 2 * T), BF16),
            pltpu.VMEM((NC, NR * T, T), BF16),
            pltpu.VMEM((NC * T, F), F32),
            pltpu.VMEM((NR, T, F), BF16),
            pltpu.VMEM((NC, T, F), BF16),
            pltpu.VMEM((NC, T, F), BF16),
            pltpu.VMEM((2, T, F), BF16),
            pltpu.VMEM((2, T, F), BF16),
            pltpu.VMEM((NC, 8, T), F32),
            pltpu.VMEM((NC, 8, T), F32),
            pltpu.VMEM((T, F), F32),
            pltpu.VMEM((T, F), F32),
            pltpu.VMEM((NC, T, F), BF16),
            pltpu.VMEM((NZ, T, F), BF16),
            pltpu.VMEM((NZ, T, F), BF16),
            pltpu.VMEM((NZ, T, F), BF16),
            pltpu.VMEM((2, T, F), BF16),
            pltpu.VMEM((2, HALF, F), BF16),
            pltpu.VMEM((4, T, F), BF16),
            pltpu.VMEM((2, F + PART, F), BF16),
            pltpu.VMEM((F + PART, F), BF16),
            pltpu.VMEM((NC, PART, F), BF16),
            pltpu.VMEM((NC, PART, F), BF16),
            pltpu.VMEM((NZ, WPART, F), BF16),
            pltpu.VMEM((NC, WPART, F), BF16),
            pltpu.VMEM((F, F), BF16),
            pltpu.VMEM((F, F), BF16),
            pltpu.VMEM((T, F), F32),
            dma((TILE_CUTS,)),
            dma,
        ]
        + [dma((NZ + 4,))] * 2
        + [dma((NZ,))] * 2
        + [dma((NC,))] * 4
        + [dma((2,))] * 2
        + [dma((NC,))] * 2
        + [dma((NZ,))] * 4
        + [dma, dma]
        + [dma((NC,))] * 2
        + [dma((NZ,))] * 2
        + [dma((NC,))] * 2
        + [dma, dma],
        compiler_params=pltpu.CompilerParams(
            collective_id=0, has_side_effects=True, vmem_limit_bytes=56 * 2**20
        ),
        name="sage_layer",
    )(
        feats,
        tiles.reshape(SLOTS, T, T),
        tile_row,
        tile_col,
        counts,
        w_self,
        w_neigh,
        bias.reshape(1, F),
        grad_out,
    )
    outs = pl.pallas_call(
        hand_over,
        out_shape=[jax.ShapeDtypeStruct(o.shape, t) for o, t in zip(outs, (BF16, BF16, F32, F32, F32))],
        in_specs=[vmem] * 5,
        out_specs=[vmem] * 5,
        name="hand_over",
    )(*outs)
    return (outs[0], outs[1], outs[2], outs[3], outs[4].reshape(F))


def solution(mesh):
    placed = (
        P(("row", "col"), None),
        P(("row", "col"), None, None, None),
        P(("row", "col"), None),
        P(("row", "col"), None),
        P(("row", "col")),
        P(),
        P(),
        P(),
        P(("row", "col"), None),
    )
    return jax.shard_map(
        per_device,
        mesh=mesh,
        in_specs=placed,
        out_specs=(P(("row", "col"), None), P(("row", "col"), None), P(), P(), P()),
        check_vma=False,
    )
```
